512 devices in a mesh: fsdp: 32 (over y, z_lo), col: 16 (over x, z_hi, core).
Axes of the slice: x: 4, y: 8, z: 8 (z_hi: 2, z_lo: 4; z = z_hi * 4 + z_lo), core: 2. Of those that a mesh axis runs over, the one named last changes fastest.
Arguments:
- joined_gradient: bfloat16 [6144, 18432], P('fsdp', 'col'), may hold values from -6 to 6
- output_gradient: bfloat16 [6144, 6144], P('fsdp', 'col'), may hold values from -6 to 6
- joined_left_basis: bfloat16 [6144, 512], P('fsdp', 'col'), may hold values from -0.078125 to 0.078125
- joined_right_basis: bfloat16 [18432, 512], P('col', 'fsdp'), may hold values from -0.046875 to 0.046875
- output_left_basis: bfloat16 [6144, 512], P('fsdp', 'col'), may hold values from -0.078125 to 0.078125
- output_right_basis: bfloat16 [6144, 512], P('col', 'fsdp'), may hold values from -0.078125 to 0.078125
- joined_left_eigen: float32 [512], replicated, may hold values from 0.05 to 20
- joined_right_eigen: float32 [512], replicated, may hold values from 0.05 to 20
- output_left_eigen: float32 [512], replicated, may hold values from 0.05 to 20
- output_right_eigen: float32 [512], replicated, may hold values from 0.05 to 20
- damping: float32 [1], replicated, may hold values from 0.5 to 1
Outputs:
- joined_update: float32 [6144, 18432], P('fsdp', 'col')
- output_update: float32 [6144, 6144], P('fsdp', 'col')
The draws below stay inside these ranges and needn't reach their ends.
All inputs are finite; a program needn't handle non-finite values.
Results may differ from the reference program's by a relative error of at most 0.0003.
Values may be sent and summed in bfloat16 or wider, within the bound.
No kernel may reach another device: no remote copies, remote signals or barrier semaphores. Data moves between devices by JAX's collectives and lax.ppermute only.
A program may use at most 64 MiB of HBM per device.

```python
import math
import jax
import jax.numpy as jnp
from jax import lax

D = 6144
K = 512
QKV = 18432


def steps_of(own_key, dims, shards, least, top_value):
    level, own = 1.0, jax.random.fold_in(own_key, 6)
    for dim, blocks in shards:
        draws = jnp.exp(jax.random.uniform(jax.random.fold_in(own, dim), (blocks,), jnp.float32, least / len(shards), top_value / len(shards)))
        level = level * jnp.repeat(draws, dims[dim] // blocks).reshape([-1 if axis == dim else 1 for axis in range(len(dims))])
    return level


def centred(own_key, extent, deviation, limit, pieces=(), dtype=jnp.bfloat16):
    entries = deviation * jax.random.normal(own_key, extent, jnp.float32)
    if pieces:
        entries = entries * steps_of(own_key, extent, pieces, -0.22, 0.18)
    return jnp.clip(entries, -limit, limit).astype(dtype)


def setup_inputs(seed: int = 0) -> dict:
    seeds = jax.random.split(jax.random.key(seed), 12)
    joined_gradient = centred(seeds[0], (D, QKV), 1.0, 6.0, ((0, 32), (1, 16)))
    output_gradient = centred(seeds[1], (D, D), 1.0, 6.0, ((0, 32), (1, 16)))
    joined_left_basis = centred(seeds[2], (D, K), D ** -0.5, 0.078125, ((0, 32), (1, 16)))
    joined_right_basis = centred(seeds[3], (QKV, K), QKV ** -0.5, 0.046875, ((0, 16), (1, 32)))
    output_left_basis = centred(seeds[4], (D, K), D ** -0.5, 0.078125, ((0, 32), (1, 16)))
    output_right_basis = centred(seeds[5], (D, K), D ** -0.5, 0.078125, ((0, 16), (1, 32)))
    joined_left_eigen = jnp.clip(jnp.exp(jax.random.uniform(seeds[6], (K,), jnp.float32, math.log(0.05), math.log(20.0))), 0.05, 20.0)
    joined_right_eigen = jnp.clip(jnp.exp(jax.random.uniform(seeds[7], (K,), jnp.float32, math.log(0.05), math.log(20.0))), 0.05, 20.0)
    output_left_eigen = jnp.clip(jnp.exp(jax.random.uniform(seeds[8], (K,), jnp.float32, math.log(0.05), math.log(20.0))), 0.05, 20.0)
    output_right_eigen = jnp.clip(jnp.exp(jax.random.uniform(seeds[9], (K,), jnp.float32, math.log(0.05), math.log(20.0))), 0.05, 20.0)
    damping = jnp.clip(jax.random.uniform(seeds[10], (1,), jnp.float32, 0.5, 1.0), 0.5, 1.0)
    return dict(joined_gradient=joined_gradient, output_gradient=output_gradient, joined_left_basis=joined_left_basis, joined_right_basis=joined_right_basis, output_left_basis=output_left_basis, output_right_basis=output_right_basis, joined_left_eigen=joined_left_eigen, joined_right_eigen=joined_right_eigen, output_left_eigen=output_left_eigen, output_right_eigen=output_right_eigen, damping=damping)


def apply_factors(gradient, left_basis, right_basis, left_eigen, right_eigen, damp):
    highest = lax.Precision.HIGHEST
    left_shift = 1.0 / (left_eigen + damp) - 1.0 / damp
    right_shift = 1.0 / (right_eigen + damp) - 1.0 / damp
    left_wide = left_basis.astype(jnp.float32)
    right_wide = right_basis.astype(jnp.float32)
    grad_wide = gradient.astype(jnp.float32)
    rows = jnp.einsum("rk,rc->kc", left_wide, grad_wide, precision=highest)
    applied = grad_wide / damp + jnp.dot(left_wide, left_shift[:, None] * rows, precision=highest)
    cols = jnp.dot(applied, right_wide, precision=highest)
    return applied / damp + jnp.einsum("rk,ck->rc", cols * right_shift[None, :], right_wide, precision=highest)


def reference(joined_gradient, output_gradient, joined_left_basis, joined_right_basis, output_left_basis, output_right_basis, joined_left_eigen, joined_right_eigen, output_left_eigen, output_right_eigen, damping):
    damp = damping[0]
    joined_update = apply_factors(joined_gradient, joined_left_basis, joined_right_basis, joined_left_eigen, joined_right_eigen, damp)
    output_update = apply_factors(output_gradient, output_left_basis, output_right_basis, output_left_eigen, output_right_eigen, damp)
    return (joined_update, output_update)
```

```python
import jax
import jax.numpy as jnp
from jax import lax
from jax.sharding import Mesh, PartitionSpec as P

FSDP = ("yp", "yb", "zp", "zb")
COL = ("x", "zh", "c")
QUAD = ("yb", "zb")
OCT = ("yp", "zp")
ROUND = (8, 7)


def shifted(eigen, damp):
    return 1.0 / (eigen + damp) - 1.0 / damp


def exchange(blocks, axes):
    return lax.all_to_all(blocks, axes, 0, 0, tiled=True)


def halves(wide):
    high = lax.reduce_precision(wide, *ROUND)
    return high.astype(jnp.bfloat16), (wide - high).astype(jnp.bfloat16)


def dot_wide_left(wide, narrow, dims):
    high, low = halves(wide)
    dot = lambda part: lax.dot_general(part, narrow, (dims, ((), ())), preferred_element_type=jnp.float32)
    return dot(high) + dot(low)


def dot_wide_right(narrow, wide, dims):
    high, low = halves(wide)
    dot = lambda part: lax.dot_general(narrow, part, (dims, ((), ())), preferred_element_type=jnp.float32)
    return dot(high) + dot(low)


def pack(values):
    top = jnp.max(jnp.abs(values))
    power = jnp.clip(jnp.floor(jnp.log2(jnp.maximum(top, 1e-30))), -100.0, 120.0)
    scaled = (values * jnp.exp2(14.0 - power)).astype(jnp.float16)
    tail = jnp.broadcast_to(power.astype(jnp.float16), values.shape[:-2] + (8, values.shape[-1]))
    return jnp.concatenate([scaled, tail], axis=-2)


def unpack(packed):
    rows = packed.shape[-2] - 8
    power = packed[..., rows : rows + 1, :].astype(jnp.float32)
    return packed[..., :rows, :].astype(jnp.float32) * jnp.exp2(power - 14.0)


def swap(values, axis):
    return lax.ppermute(values, axis, [(0, 1), (1, 0)])


def around(values, axis, size, step):
    return lax.ppermute(values, axis, [(i, (i + step) % size) for i in range(size)])


def quad_sum(values, quad):
    first = lax.ppermute(values, QUAD, [(0, 1), (1, 2), (2, 0)])
    second = lax.ppermute(values, QUAD, [(0, 2), (1, 0), (2, 1)])
    return values + first + second


def col_sum(values):
    values = values + swap(values, "c")
    values = values + swap(values, "zh")
    return values + around(values, "x", 4, 1) + around(values, "x", 4, 2) + around(values, "x", 4, 3)


def core_part(values, core, own):
    half = values.shape[0] // 2
    return lax.dynamic_slice_in_dim(values, (core if own else 1 - core) * half, half, 0)


def joined_pair(mine, other, place):
    first = jnp.where(place == 0, mine, other)
    second = jnp.where(place == 0, other, mine)
    return jnp.concatenate([first, second], axis=0)


def local(
    joined_gradient,
    output_gradient,
    joined_left_basis,
    joined_right_basis,
    output_left_basis,
    output_right_basis,
    joined_left_eigen,
    joined_right_eigen,
    output_left_eigen,
    output_right_eigen,
    damping,
):
    damp = damping[0]
    quad = lax.axis_index("yb") * 2 + lax.axis_index("zb")
    octant = lax.axis_index("yp") * 2 + lax.axis_index("zp")
    core, high = lax.axis_index("c"), lax.axis_index("zh")
    is_output = quad == 3
    left_shift = shifted(jnp.where(is_output, output_left_eigen, joined_left_eigen), damp)
    right_shift = shifted(jnp.where(is_output, output_right_eigen, joined_right_eigen), damp)
    left_shift = left_shift.reshape(8, 2, 32).transpose(1, 0, 2).reshape(512)
    own_shift = lax.dynamic_slice_in_dim(left_shift, octant * 64, 64, 0)

    gradient = jnp.stack(
        [joined_gradient[:, :384], joined_gradient[:, 384:768], joined_gradient[:, 768:], output_gradient]
    )
    gradient = exchange(gradient, QUAD)

    left_j, left_o = joined_left_basis.T, output_left_basis.T
    left = jnp.stack([left_j, left_j, left_j, left_o])
    left = jnp.broadcast_to(left[:, None], (4, 8, 32, 192)).reshape(32, 32, 192)
    left = exchange(left, QUAD + ("x", "zh")).reshape(4, 256, 192)
    left = lax.all_gather(left, "c", axis=1, tiled=True)

    right = jnp.stack(
        [joined_right_basis.T[:, :384], joined_right_basis.T[:, 384:768], joined_right_basis.T[:, 768:], output_right_basis.T]
    )
    right = jnp.broadcast_to(right.reshape(1, 2, 1, 2, 16, 384), (4, 2, 2, 2, 16, 384)).reshape(32, 16, 384)
    right = exchange(right, FSDP).reshape(512, 384)

    rows = sum(
        jnp.dot(left[q], gradient[q], preferred_element_type=jnp.float32) for q in range(4)
    )
    rows = exchange(pack(rows.reshape(8, 64, 384)), OCT)
    rows = jnp.sum(unpack(rows), axis=0)

    core_sum = dot_wide_left(rows, right, ((1,), (1,)))
    core_sum = quad_sum(col_sum(core_sum), quad)
    mixed = rows / damp + dot_wide_left(core_sum * right_shift[None, :], right, ((1,), (0,)))
    mixed = mixed * own_shift[:, None]
    packed = pack(mixed)
    mixed = unpack(exchange(jnp.broadcast_to(packed[None], (8, 72, 384)), OCT)).reshape(512, 384)

    whole = gradient.reshape(768, 384)
    cols = lax.dot_general(whole, right, (((1,), (1,)), ((), ())), preferred_element_type=jnp.float32)
    cols = core_part(cols, core, True) + swap(core_part(cols, core, False), "c")
    cols = jnp.sum(exchange(cols.reshape(4, 96, 512), ("x",)), axis=0)
    cols = core_part(cols, high, True) + swap(core_part(cols, high, False), "zh")
    cols = quad_sum(cols, quad)
    cols = joined_pair(cols, swap(cols, "zh"), high)
    cols = exchange(jnp.broadcast_to(cols[None], (4, 96, 512)), ("x",)).reshape(384, 512)
    cols = joined_pair(cols, swap(cols, "c"), core)

    part = dot_wide_left(cols * (right_shift / damp)[None, :], right, ((1,), (0,))).reshape(4, 192, 384)
    high_mixed, low_mixed = halves(mixed)
    pieces = []
    for q in range(4):
        dot = lambda m: lax.dot_general(left[q], m, (((0,), (0,)), ((), ())), preferred_element_type=jnp.float32)
        pieces.append(part[q] + dot(high_mixed) + dot(low_mixed))
    update = unpack(exchange(pack(jnp.stack(pieces)), QUAD))
    square = damp * damp
    joined_update = jnp.concatenate([update[0], update[1], update[2]], axis=1) + joined_gradient.astype(jnp.float32) / damp / damp
    output_update = update[3] + output_gradient.astype(jnp.float32) / damp / damp
    return joined_update, output_update


def solution(mesh):
    fine = Mesh(mesh.devices.reshape(4, 2, 2, 2, 4, 2, 2), ("yp", "yb", "zp", "zb", "x", "zh", "c"))
    placed = (
        P(FSDP, COL),
        P(FSDP, COL),
        P(FSDP, COL),
        P(COL, FSDP),
        P(FSDP, COL),
        P(COL, FSDP),
        P(),
        P(),
        P(),
        P(),
        P(),
    )
    return jax.shard_map(
        local,
        mesh=fine,
        in_specs=placed,
        out_specs=(P(FSDP, COL), P(FSDP, COL)),
        check_vma=False,
    )
```

```python
import jax
import jax.numpy as jnp
from jax import lax
from jax.sharding import Mesh, PartitionSpec as P

FSDP = ("yp", "yb", "zp", "zb")
COL = ("x", "zh", "c")
QUAD = ("yb", "zb")
OCT = ("yp", "zp")
ROUND = (8, 7)


def shifted(eigen, damp):
    return 1.0 / (eigen + damp) - 1.0 / damp


def exchange(blocks, axes):
    return lax.all_to_all(blocks, axes, 0, 0, tiled=True)


def halves(wide):
    high = lax.reduce_precision(wide, *ROUND)
    return high.astype(jnp.bfloat16), (wide - high).astype(jnp.bfloat16)


def dot_wide_left(wide, narrow, dims):
    high, low = halves(wide)
    dot = lambda part: lax.dot_general(part, narrow, (dims, ((), ())), preferred_element_type=jnp.float32)
    return dot(high) + dot(low)


def dot_wide_right(narrow, wide, dims):
    high, low = halves(wide)
    dot = lambda part: lax.dot_general(narrow, part, (dims, ((), ())), preferred_element_type=jnp.float32)
    return dot(high) + dot(low)


def pack(values):
    top = jnp.max(jnp.abs(values))
    power = jnp.clip(jnp.floor(jnp.log2(jnp.maximum(top, 1e-30))), -100.0, 120.0)
    scaled = (values * jnp.exp2(14.0 - power)).astype(jnp.float16)
    tail = jnp.broadcast_to(power.astype(jnp.float16), values.shape[:-2] + (8, values.shape[-1]))
    return jnp.concatenate([scaled, tail], axis=-2)


def unpack(packed):
    rows = packed.shape[-2] - 8
    power = packed[..., rows : rows + 1, :].astype(jnp.float32)
    return packed[..., :rows, :].astype(jnp.float32) * jnp.exp2(power - 14.0)


def swap(values, axis):
    return lax.ppermute(values, axis, [(0, 1), (1, 0)])


def around(values, axis, size, step):
    return lax.ppermute(values, axis, [(i, (i + step) % size) for i in range(size)])


def quad_sum(values, quad):
    first = lax.ppermute(values, QUAD, [(0, 1), (1, 2), (2, 0)])
    second = lax.ppermute(values, QUAD, [(0, 2), (1, 0), (2, 1)])
    return values + first + second


def col_sum(values):
    values = values + swap(values, "c")
    values = values + swap(values, "zh")
    return values + around(values, "x", 4, 1) + around(values, "x", 4, 2) + around(values, "x", 4, 3)


def core_part(values, core, own):
    half = values.shape[0] // 2
    return lax.dynamic_slice_in_dim(values, (core if own else 1 - core) * half, half, 0)


def joined_pair(mine, other, place):
    first = jnp.where(place == 0, mine, other)
    second = jnp.where(place == 0, other, mine)
    return jnp.concatenate([first, second], axis=0)


def local(
    joined_gradient,
    output_gradient,
    joined_left_basis,
    joined_right_basis,
    output_left_basis,
    output_right_basis,
    joined_left_eigen,
    joined_right_eigen,
    output_left_eigen,
    output_right_eigen,
    damping,
):
    damp = damping[0]
    quad = lax.axis_index("yb") * 2 + lax.axis_index("zb")
    octant = lax.axis_index("yp") * 2 + lax.axis_index("zp")
    core, high = lax.axis_index("c"), lax.axis_index("zh")
    is_output = quad == 3
    left_shift = shifted(jnp.where(is_output, output_left_eigen, joined_left_eigen), damp)
    right_shift = shifted(jnp.where(is_output, output_right_eigen, joined_right_eigen), damp)
    left_shift = left_shift.reshape(8, 2, 32).transpose(1, 0, 2).reshape(512)
    right_shift = right_shift.reshape(4, 2, 2, 2, 16).transpose(0, 2, 1, 3, 4).reshape(512)
    own_shift = lax.dynamic_slice_in_dim(left_shift, octant * 64, 64, 0)

    left_j, left_o = joined_left_basis.T, output_left_basis.T
    right_j, right_o = joined_right_basis.T, output_right_basis.T
    gradients = (joined_gradient[:, :384], joined_gradient[:, 384:768], joined_gradient[:, 768:], output_gradient)
    rights = (right_j[:, :384], right_j[:, 384:768], right_j[:, 768:], right_o)
    lefts = [jnp.concatenate([left[:16], left[16:]], axis=1) for left in (left_j, left_o)]
    lefts = (lefts[0], lefts[0], lefts[0], lefts[1])
    sent = jnp.stack([jnp.concatenate(three, axis=0) for three in zip(gradients, rights, lefts)])
    got = exchange(sent, QUAD)
    gradient = got[:, :192].reshape(768, 384)

    left = jnp.concatenate([got[:, 208:, :192], got[:, 208:, 192:]], axis=1)
    left = left.transpose(1, 0, 2).reshape(32, 768)
    left = exchange(jnp.broadcast_to(left[None], (8, 32, 768)), ("x", "zh")).reshape(256, 768)
    left = lax.all_gather(left, "c", axis=0, tiled=True)

    right = got[:, 192:208].reshape(64, 384)
    right = exchange(jnp.broadcast_to(right[None], (8, 64, 384)), OCT).reshape(512, 384)

    rows = jnp.dot(left, gradient, preferred_element_type=jnp.float32)
    rows = exchange(pack(rows.reshape(8, 64, 384)), OCT)
    rows = jnp.sum(unpack(rows), axis=0)

    core_sum = dot_wide_left(rows, right, ((1,), (1,)))
    core_sum = quad_sum(col_sum(core_sum), quad)
    mixed = rows / damp + dot_wide_left(core_sum * right_shift[None, :], right, ((1,), (0,)))
    mixed = mixed * own_shift[:, None]
    packed = pack(mixed)
    mixed = unpack(exchange(jnp.broadcast_to(packed[None], (8, 72, 384)), OCT)).reshape(512, 384)

    cols = lax.dot_general(gradient, right, (((1,), (1,)), ((), ())), preferred_element_type=jnp.float32)
    cols = core_part(cols, core, True) + swap(core_part(cols, core, False), "c")
    cols = jnp.sum(exchange(cols.reshape(4, 96, 512), ("x",)), axis=0)
    cols = core_part(cols, high, True) + swap(core_part(cols, high, False), "zh")
    cols = quad_sum(cols, quad)
    cols = joined_pair(cols, swap(cols, "zh"), high)
    cols = exchange(jnp.broadcast_to(cols[None], (4, 96, 512)), ("x",)).reshape(384, 512)
    cols = joined_pair(cols, swap(cols, "c"), core)

    part = dot_wide_left(cols * (right_shift / damp)[None, :], right, ((1,), (0,)))
    update = part + dot_wide_right(left, mixed, ((0,), (0,)))
    update = unpack(exchange(pack(update.reshape(4, 192, 384)), QUAD))
    joined_update = jnp.concatenate([update[0], update[1], update[2]], axis=1) + joined_gradient.astype(jnp.float32) / damp / damp
    output_update = update[3] + output_gradient.astype(jnp.float32) / damp / damp
    return joined_update, output_update


def solution(mesh):
    fine = Mesh(mesh.devices.reshape(4, 2, 2, 2, 4, 2, 2), ("yp", "yb", "zp", "zb", "x", "zh", "c"))
    placed = (
        P(FSDP, COL),
        P(FSDP, COL),
        P(FSDP, COL),
        P(COL, FSDP),
        P(FSDP, COL),
        P(COL, FSDP),
        P(),
        P(),
        P(),
        P(),
        P(),
    )
    return jax.shard_map(
        local,
        mesh=fine,
        in_specs=placed,
        out_specs=(P(FSDP, COL), P(FSDP, COL)),
        check_vma=False,
    )
```

```python
import jax
import jax.numpy as jnp
from jax import lax
from jax.sharding import Mesh, PartitionSpec as P

FSDP = ("yp", "yb", "zp", "zb")
COL = ("x", "zh", "c")
QUAD = ("yb", "zb")
OCT = ("yp", "zp")
ROUND = (8, 7)


def shifted(eigen, damp):
    return 1.0 / (eigen + damp) - 1.0 / damp


def exchange(blocks, axes):
    return lax.all_to_all(blocks, axes, 0, 0, tiled=True)


def halves(wide):
    high = lax.reduce_precision(wide, *ROUND)
    return high.astype(jnp.bfloat16), (wide - high).astype(jnp.bfloat16)


def dot_wide_left(wide, narrow, dims):
    high, low = halves(wide)
    dot = lambda part: lax.dot_general(part, narrow, (dims, ((), ())), preferred_element_type=jnp.float32)
    return dot(high) + dot(low)


def dot_wide_right(narrow, wide, dims):
    high, low = halves(wide)
    dot = lambda part: lax.dot_general(narrow, part, (dims, ((), ())), preferred_element_type=jnp.float32)
    return dot(high) + dot(low)


def pack(values):
    top = jnp.max(jnp.abs(values))
    power = jnp.clip(jnp.floor(jnp.log2(jnp.maximum(top, 1e-30))), -100.0, 120.0)
    scaled = (values * jnp.exp2(14.0 - power)).astype(jnp.float16)
    tail = jnp.broadcast_to(power.astype(jnp.float16), values.shape[:-2] + (8, values.shape[-1]))
    return jnp.concatenate([scaled, tail], axis=-2)


def unpack(packed):
    rows = packed.shape[-2] - 8
    power = packed[..., rows : rows + 1, :].astype(jnp.float32)
    return packed[..., :rows, :].astype(jnp.float32) * jnp.exp2(power - 14.0)


def swap(values, axis):
    return lax.ppermute(values, axis, [(0, 1), (1, 0)])


def around(values, axis, size, step):
    return lax.ppermute(values, axis, [(i, (i + step) % size) for i in range(size)])


def quad_sum(values, quad):
    first = lax.ppermute(values, QUAD, [(0, 1), (1, 2), (2, 0)])
    second = lax.ppermute(values, QUAD, [(0, 2), (1, 0), (2, 1)])
    return values + first + second


def ring_parts(values, place):
    total = lax.dynamic_index_in_dim(values, place, 0, False)
    for step in (1, 2, 3):
        block = lax.dynamic_index_in_dim(values, (place + step) % 4, 0, False)
        total = total + around(block, "x", 4, step)
    return total


def ring_gather(values, place):
    held = jnp.stack([values] + [around(values, "x", 4, step) for step in (1, 2, 3)])
    return jnp.concatenate([lax.dynamic_index_in_dim(held, (place - j) % 4, 0, False) for j in range(4)], axis=0)


def core_part(values, core, own):
    half = values.shape[0] // 2
    return lax.dynamic_slice_in_dim(values, (core if own else 1 - core) * half, half, 0)


def joined_pair(mine, other, place):
    first = jnp.where(place == 0, mine, other)
    second = jnp.where(place == 0, other, mine)
    return jnp.concatenate([first, second], axis=0)


def local(
    joined_gradient,
    output_gradient,
    joined_left_basis,
    joined_right_basis,
    output_left_basis,
    output_right_basis,
    joined_left_eigen,
    joined_right_eigen,
    output_left_eigen,
    output_right_eigen,
    damping,
):
    damp = damping[0]
    quad = lax.axis_index("yb") * 2 + lax.axis_index("zb")
    octant = lax.axis_index("yp") * 2 + lax.axis_index("zp")
    core, high, place = lax.axis_index("c"), lax.axis_index("zh"), lax.axis_index("x")
    is_output = quad == 3
    left_shift = shifted(jnp.where(is_output, output_left_eigen, joined_left_eigen), damp)
    right_shift = shifted(jnp.where(is_output, output_right_eigen, joined_right_eigen), damp)
    left_shift = left_shift.reshape(8, 2, 32).transpose(1, 0, 2).reshape(512)
    right_shift = right_shift.reshape(4, 2, 2, 2, 16).transpose(0, 2, 1, 3, 4).reshape(4, 2, 64)[::-1]
    right_shift = jnp.where(lax.axis_index("zp") == 1, right_shift[:, ::-1], right_shift)
    right_shift = jnp.concatenate([right_shift, right_shift], axis=0)
    right_shift = lax.dynamic_slice_in_dim(right_shift, 3 - lax.axis_index("yp"), 4, 0).reshape(512)
    own_shift = lax.dynamic_slice_in_dim(left_shift, octant * 64, 64, 0)

    left_j, left_o = joined_left_basis.T, output_left_basis.T
    right_j, right_o = joined_right_basis.T, output_right_basis.T
    gradients = (joined_gradient[:, :384], joined_gradient[:, 384:768], joined_gradient[:, 768:], output_gradient)
    rights = (right_j[:, :384], right_j[:, 384:768], right_j[:, 768:], right_o)
    lefts = [jnp.concatenate([left[:16], left[16:]], axis=1) for left in (left_j, left_o)]
    lefts = (lefts[0], lefts[0], lefts[0], lefts[1])
    sent = jnp.stack([jnp.concatenate(three, axis=0) for three in zip(gradients, rights, lefts)])
    got = exchange(sent, QUAD)
    gradient = got[:, :192].reshape(768, 384)

    left = jnp.concatenate([got[:, 208:, :192], got[:, 208:, 192:]], axis=1)
    left = left.transpose(1, 0, 2).reshape(32, 768)
    left = exchange(jnp.broadcast_to(left[None], (8, 32, 768)), ("x", "zh")).reshape(256, 768)
    left = lax.all_gather(left, "c", axis=0, tiled=True)

    right = got[:, 192:208].reshape(64, 384)
    right = jnp.concatenate([right, swap(right, "zp")], axis=0)
    right = jnp.concatenate([right] + [around(right, "yp", 4, step) for step in (1, 2, 3)], axis=0)

    rows = jnp.dot(left, gradient, preferred_element_type=jnp.float32)
    rows = exchange(pack(rows.reshape(8, 64, 384)), OCT)
    rows = jnp.sum(unpack(rows), axis=0)

    cols = lax.dot_general(gradient, right, (((1,), (1,)), ((), ())), preferred_element_type=jnp.float32)
    cols = core_part(cols, core, True) + swap(core_part(cols, core, False), "c")
    cols = ring_parts(cols.reshape(4, 96, 512), place)

    core_sum = dot_wide_left(rows, right, ((1,), (1,)))
    core_sum = core_sum + swap(core_sum, "c")
    both = swap(jnp.concatenate([core_sum, core_part(cols, high, False)], axis=0), "zh")
    core_sum = core_sum + both[:64]
    cols = core_part(cols, high, True) + both[64:]
    core_sum = core_sum + around(core_sum, "x", 4, 1) + around(core_sum, "x", 4, 2) + around(core_sum, "x", 4, 3)
    both = quad_sum(jnp.concatenate([core_sum, cols], axis=0), quad)
    core_sum, cols = both[:64], both[64:]
    mixed = rows / damp + dot_wide_left(core_sum * right_shift[None, :], right, ((1,), (0,)))
    mixed = mixed * own_shift[:, None]
    packed = pack(mixed)
    mixed = unpack(exchange(jnp.broadcast_to(packed[None], (8, 72, 384)), OCT)).reshape(512, 384)

    cols = joined_pair(cols, swap(cols, "zh"), high)
    cols = ring_gather(cols, place)
    cols = joined_pair(cols, swap(cols, "c"), core)

    part = dot_wide_left(cols * (right_shift / damp)[None, :], right, ((1,), (0,)))
    update = part + dot_wide_right(left, mixed, ((0,), (0,)))
    update = unpack(exchange(pack(update.reshape(4, 192, 384)), QUAD))
    joined_update = jnp.concatenate([update[0], update[1], update[2]], axis=1) + joined_gradient.astype(jnp.float32) / damp / damp
    output_update = update[3] + output_gradient.astype(jnp.float32) / damp / damp
    return joined_update, output_update


def solution(mesh):
    fine = Mesh(mesh.devices.reshape(4, 2, 2, 2, 4, 2, 2), ("yp", "yb", "zp", "zb", "x", "zh", "c"))
    placed = (
        P(FSDP, COL),
        P(FSDP, COL),
        P(FSDP, COL),
        P(COL, FSDP),
        P(FSDP, COL),
        P(COL, FSDP),
        P(),
        P(),
        P(),
        P(),
        P(),
    )
    return jax.shard_map(
        local,
        mesh=fine,
        in_specs=placed,
        out_specs=(P(FSDP, COL), P(FSDP, COL)),
        check_vma=False,
    )
```

```python
import jax
import jax.numpy as jnp
from jax import lax
from jax.sharding import Mesh, PartitionSpec as P

FSDP = ("yp", "yb", "zp", "zb")
COL = ("x", "zh", "c")
QUAD = ("yb", "zb")
OCT = ("yp", "zp")
ROUND = (8, 7)


def shifted(eigen, damp):
    return 1.0 / (eigen + damp) - 1.0 / damp


def exchange(blocks, axes):
    return lax.all_to_all(blocks, axes, 0, 0, tiled=True)


def halves(wide):
    high = lax.reduce_precision(wide, *ROUND)
    return high.astype(jnp.bfloat16), (wide - high).astype(jnp.bfloat16)


def dot_wide_left(wide, narrow, dims):
    high, low = halves(wide)
    dot = lambda part: lax.dot_general(part, narrow, (dims, ((), ())), preferred_element_type=jnp.float32)
    return dot(high) + dot(low)


def dot_wide_right(narrow, wide, dims):
    high, low = halves(wide)
    dot = lambda part: lax.dot_general(narrow, part, (dims, ((), ())), preferred_element_type=jnp.float32)
    return dot(high) + dot(low)


def pack(values):
    top = jnp.max(jnp.abs(values))
    power = jnp.clip(jnp.floor(jnp.log2(jnp.maximum(top, 1e-30))), -100.0, 120.0)
    scaled = (values * jnp.exp2(14.0 - power)).astype(jnp.float16)
    tail = jnp.broadcast_to(power.astype(jnp.float16), values.shape[:-2] + (8, values.shape[-1]))
    return jnp.concatenate([scaled, tail], axis=-2)


def unpack(packed):
    rows = packed.shape[-2] - 8
    power = packed[..., rows : rows + 1, :].astype(jnp.float32)
    return packed[..., :rows, :].astype(jnp.float32) * jnp.exp2(power - 14.0)


def swap(values, axis):
    return lax.ppermute(values, axis, [(0, 1), (1, 0)])


def around(values, axis, size, step):
    return lax.ppermute(values, axis, [(i, (i + step) % size) for i in range(size)])


def quad_sum(values, quad):
    first = lax.ppermute(values, QUAD, [(0, 1), (1, 2), (2, 0)])
    second = lax.ppermute(values, QUAD, [(0, 2), (1, 0), (2, 1)])
    return values + first + second


def ring_gather(values, place):
    held = jnp.stack([values] + [around(values, "x", 4, step) for step in (1, 2, 3)])
    return jnp.concatenate([lax.dynamic_index_in_dim(held, (place - j) % 4, 0, False) for j in range(4)], axis=0)


def core_part(values, core, own):
    half = values.shape[0] // 2
    return lax.dynamic_slice_in_dim(values, (core if own else 1 - core) * half, half, 0)


def joined_pair(mine, other, place):
    first = jnp.where(place == 0, mine, other)
    second = jnp.where(place == 0, other, mine)
    return jnp.concatenate([first, second], axis=0)


def local(
    joined_gradient,
    output_gradient,
    joined_left_basis,
    joined_right_basis,
    output_left_basis,
    output_right_basis,
    joined_left_eigen,
    joined_right_eigen,
    output_left_eigen,
    output_right_eigen,
    damping,
):
    damp = damping[0]
    quad = lax.axis_index("yb") * 2 + lax.axis_index("zb")
    octant = lax.axis_index("yp") * 2 + lax.axis_index("zp")
    core, place = lax.axis_index("c"), lax.axis_index("x")
    is_output = quad == 3
    left_shift = shifted(jnp.where(is_output, output_left_eigen, joined_left_eigen), damp)
    right_shift = shifted(jnp.where(is_output, output_right_eigen, joined_right_eigen), damp)
    left_shift = left_shift.reshape(8, 2, 32).transpose(1, 0, 2).reshape(512)
    right_shift = right_shift.reshape(4, 2, 2, 2, 16).transpose(0, 2, 1, 3, 4).reshape(4, 2, 64)[::-1]
    right_shift = jnp.where(lax.axis_index("zp") == 1, right_shift[:, ::-1], right_shift)
    right_shift = jnp.concatenate([right_shift, right_shift], axis=0)
    right_shift = lax.dynamic_slice_in_dim(right_shift, 3 - lax.axis_index("yp"), 4, 0).reshape(512)
    own_shift = lax.dynamic_slice_in_dim(left_shift, octant * 64, 64, 0)

    left_j, left_o = joined_left_basis.T, output_left_basis.T
    left = jnp.stack([left_j, left_j, left_j, left_o])
    left = jnp.broadcast_to(left[:, None], (4, 8, 32, 192)).reshape(32, 32, 192)
    left = exchange(left, QUAD + ("x", "zh")).reshape(4, 256, 192)
    left = jnp.concatenate([left[0], left[1], left[2], left[3]], axis=1)
    left = lax.all_gather(left, "c", axis=0, tiled=True)

    right_j, right_o = joined_right_basis.T, output_right_basis.T
    gradients = (joined_gradient[:, :384], joined_gradient[:, 384:768], joined_gradient[:, 768:], output_gradient)
    rights = (right_j[:, :384], right_j[:, 384:768], right_j[:, 768:], right_o)
    sent = jnp.stack([jnp.concatenate(pair, axis=0) for pair in zip(gradients, rights)])
    got = [lax.dynamic_index_in_dim(sent, quad, 0, False)]
    for mask in (1, 2, 3):
        block = lax.dynamic_index_in_dim(sent, quad ^ mask, 0, False)
        got.append(lax.ppermute(block, QUAD, [(i, i ^ mask) for i in range(4)]))
    got = jnp.stack(got)
    got = jnp.stack([lax.dynamic_index_in_dim(got, quad ^ j, 0, False) for j in range(4)])
    gradient = got[:, :192].reshape(768, 384)
    right = got[:, 192:].reshape(64, 384)
    right = jnp.concatenate([right, swap(right, "zp")], axis=0)

    rows = jnp.dot(left, gradient, preferred_element_type=jnp.float32)
    rows = pack(rows.reshape(8, 64, 384))
    right = right + (rows[0, 0, :1] * 0).astype(jnp.bfloat16)
    rows = jnp.sum(unpack(exchange(rows, OCT)), axis=0)
    right = jnp.concatenate([right] + [around(right, "yp", 4, step) for step in (1, 2, 3)], axis=0)

    cols = lax.dot_general(gradient, right, (((1,), (1,)), ((), ())), preferred_element_type=jnp.float32)
    cols = core_part(cols, core, True) + swap(core_part(cols, core, False), "c")
    cols = cols.reshape(4, 96, 512)

    mid = dot_wide_left(rows, right, ((1,), (1,)))
    mid = core_part(mid, core, True) + swap(core_part(mid, core, False), "c")
    both = jnp.concatenate([mid, lax.dynamic_index_in_dim(cols, place, 0, False)], axis=0)
    for step in (1, 2, 3):
        block = lax.dynamic_index_in_dim(cols, (place + step) % 4, 0, False)
        both = both + around(jnp.concatenate([mid, block], axis=0), "x", 4, step)
    both = both + swap(both, "zh")
    both = quad_sum(both, quad)
    mid = lax.all_gather(both[:32], "c", axis=0, tiled=True)
    cols = both[32:]
    mixed = rows / damp + dot_wide_left(mid * right_shift[None, :], right, ((1,), (0,)))
    mixed = mixed * own_shift[:, None]
    packed = pack(mixed)
    mixed = unpack(exchange(jnp.broadcast_to(packed[None], (8, 72, 384)), OCT)).reshape(512, 384)

    cols = ring_gather(cols, place)
    cols = joined_pair(cols, swap(cols, "c"), core)

    part = dot_wide_left(cols * (right_shift / damp)[None, :], right, ((1,), (0,)))
    update = part + dot_wide_right(left, mixed, ((0,), (0,)))
    update = unpack(exchange(pack(update.reshape(4, 192, 384)), QUAD))
    joined_update = jnp.concatenate([update[0], update[1], update[2]], axis=1) + joined_gradient.astype(jnp.float32) / damp / damp
    output_update = update[3] + output_gradient.astype(jnp.float32) / damp / damp
    return joined_update, output_update


def solution(mesh):
    fine = Mesh(mesh.devices.reshape(4, 2, 2, 2, 4, 2, 2), ("yp", "yb", "zp", "zb", "x", "zh", "c"))
    placed = (
        P(FSDP, COL),
        P(FSDP, COL),
        P(FSDP, COL),
        P(COL, FSDP),
        P(FSDP, COL),
        P(COL, FSDP),
        P(),
        P(),
        P(),
        P(),
        P(),
    )
    return jax.shard_map(
        local,
        mesh=fine,
        in_specs=placed,
        out_specs=(P(FSDP, COL), P(FSDP, COL)),
        check_vma=False,
    )
```

```python
import jax
import jax.numpy as jnp
from jax import lax
from jax.sharding import Mesh, PartitionSpec as P

FSDP = ("yp", "yb", "zp", "zb")
COL = ("x", "zh", "c")
QUAD = ("yb", "zb")
OCT = ("yp", "zp")
ROUND = (8, 7)


def shifted(eigen, damp):
    return 1.0 / (eigen + damp) - 1.0 / damp


def exchange(blocks, axes):
    return lax.all_to_all(blocks, axes, 0, 0, tiled=True)


def halves(wide):
    high = lax.reduce_precision(wide, *ROUND)
    return high.astype(jnp.bfloat16), (wide - high).astype(jnp.bfloat16)


def dot_wide_left(wide, narrow, dims):
    high, low = halves(wide)
    dot = lambda part: lax.dot_general(part, narrow, (dims, ((), ())), preferred_element_type=jnp.float32)
    return dot(high) + dot(low)


def dot_wide_right(narrow, wide, dims):
    high, low = halves(wide)
    dot = lambda part: lax.dot_general(narrow, part, (dims, ((), ())), preferred_element_type=jnp.float32)
    return dot(high) + dot(low)


def pack(values, power):
    scaled = (values * jnp.exp2(14.0 - power)).astype(jnp.float16)
    tail = jnp.broadcast_to(power.astype(jnp.float16), values.shape[:-2] + (8, values.shape[-1]))
    return jnp.concatenate([scaled, tail], axis=-2)


def unpack(packed):
    rows = packed.shape[-2] - 8
    power = packed[..., rows : rows + 1, :].astype(jnp.float32)
    return packed[..., :rows, :].astype(jnp.float32) * jnp.exp2(power - 14.0)


def power_of(bound):
    return jnp.clip(jnp.floor(jnp.log2(jnp.maximum(bound, 1e-30))) + 1.0, -100.0, 120.0)


def top(values):
    return jnp.max(jnp.abs(values)).astype(jnp.float32)


def swap(values, axis):
    return lax.ppermute(values, axis, [(0, 1), (1, 0)])


def around(values, axis, size, step):
    return lax.ppermute(values, axis, [(i, (i + step) % size) for i in range(size)])


def ring_gather(values, place):
    held = jnp.stack([values] + [around(values, "x", 4, step) for step in (1, 2, 3)])
    return jnp.concatenate([lax.dynamic_index_in_dim(held, (place - j) % 4, 0, False) for j in range(4)], axis=0)


def core_part(values, core, own):
    half = values.shape[0] // 2
    return lax.dynamic_slice_in_dim(values, (core if own else 1 - core) * half, half, 0)


def joined_pair(mine, other, place):
    first = jnp.where(place == 0, mine, other)
    second = jnp.where(place == 0, other, mine)
    return jnp.concatenate([first, second], axis=0)


def local(
    joined_gradient,
    output_gradient,
    joined_left_basis,
    joined_right_basis,
    output_left_basis,
    output_right_basis,
    joined_left_eigen,
    joined_right_eigen,
    output_left_eigen,
    output_right_eigen,
    damping,
):
    damp = damping[0]
    quad = lax.axis_index("yb") * 2 + lax.axis_index("zb")
    octant = lax.axis_index("yp") * 2 + lax.axis_index("zp")
    core, place = lax.axis_index("c"), lax.axis_index("x")
    is_output = quad == 3
    left_shift = shifted(jnp.where(is_output, output_left_eigen, joined_left_eigen), damp)
    right_shift = shifted(jnp.where(is_output, output_right_eigen, joined_right_eigen), damp)
    left_shift = left_shift.reshape(8, 2, 32).transpose(1, 0, 2).reshape(512)
    right_shift = right_shift.reshape(4, 2, 2, 2, 16).transpose(0, 1, 3, 2, 4).reshape(4, 4, 2, 16)
    right_shift = jnp.where(lax.axis_index("zp") == 1, right_shift[:, :, ::-1], right_shift).reshape(512)
    own_shift = lax.dynamic_slice_in_dim(left_shift, octant * 64, 64, 0)

    left_j, left_o = joined_left_basis.T, output_left_basis.T
    left = jnp.stack([left_j, left_j, left_j, left_o])
    left = jnp.broadcast_to(left[:, None], (4, 8, 32, 192)).reshape(32, 32, 192)
    left = exchange(left, QUAD + ("x", "zh")).reshape(4, 256, 192)
    left = jnp.concatenate([left[0], left[1], left[2], left[3]], axis=1)
    left = lax.all_gather(left, "c", axis=0, tiled=True)

    right = jnp.concatenate([joined_right_basis.T, output_right_basis.T], axis=1)
    right = jnp.concatenate([right, swap(right, "zp")], axis=0)
    gradients = (joined_gradient[:, :384], joined_gradient[:, 384:768], joined_gradient[:, 768:], output_gradient)
    sent = jnp.stack(
        [jnp.concatenate([block, right[:, 384 * j : 384 * j + 384]], axis=0) for j, block in enumerate(gradients)]
    )
    got = [lax.dynamic_index_in_dim(sent, quad, 0, False)]
    for mask in (1, 2, 3):
        block = lax.dynamic_index_in_dim(sent, quad ^ mask, 0, False)
        got.append(lax.ppermute(block, QUAD, [(i, i ^ mask) for i in range(4)]))
    got = jnp.stack(got)
    got = jnp.stack([lax.dynamic_index_in_dim(got, quad ^ j, 0, False) for j in range(4)])
    gradient = got[:, :192].reshape(768, 384)
    right = got[:, 192:].reshape(128, 384)
    right = exchange(jnp.broadcast_to(right[None], (4, 128, 384)), "yp").reshape(512, 384)
    most = top(gradient)

    rows = jnp.dot(left, gradient, preferred_element_type=jnp.float32)
    rows = pack(rows.reshape(8, 64, 384), power_of(most * 60.0))
    rows = jnp.sum(unpack(exchange(rows, OCT)), axis=0)

    cols = lax.dot_general(gradient, right, (((1,), (1,)), ((), ())), preferred_element_type=jnp.float32)
    cols = core_part(cols, core, True) + swap(core_part(cols, core, False), "c")
    cols = cols.reshape(4, 96, 512)

    mid = dot_wide_left(rows, right, ((1,), (1,)))
    other = jnp.concatenate([core_part(mid, core, False), jnp.broadcast_to(most, (8, 512))], axis=0)
    other = swap(other, "c")
    mid = (core_part(mid, core, True) + other[:32]) / 512.0
    power = power_of(jnp.maximum(most, other[32, 0]) * 864.0)
    both = jnp.concatenate([jnp.broadcast_to(mid[None], (4, 32, 512)), cols], axis=1)
    both = exchange(pack(both, power), "x")
    power = jnp.max(both[:, 128, 0]).astype(jnp.float32)
    both = jnp.sum(unpack(both), axis=0)
    got = swap(pack(both, power), "zh")
    power = jnp.maximum(power, got[128, 0].astype(jnp.float32))
    both = both + unpack(got)
    both = exchange(jnp.broadcast_to(pack(both, power)[None], (4, 136, 512)), QUAD)
    power = jnp.max(both[:, 128, 0]).astype(jnp.float32)
    same = (lax.broadcasted_iota(jnp.int32, (4, 1, 1), 0) == 3) == is_output
    both = jnp.sum(jnp.where(same, unpack(both), 0.0), axis=0)
    mid = lax.all_gather(both[:32], "c", axis=0, tiled=True) * 512.0
    cols = (both[32:] * jnp.exp2(14.0 - power)).astype(jnp.float16)
    mixed = rows / damp + dot_wide_left(mid * right_shift[None, :], right, ((1,), (0,)))
    mixed = mixed * own_shift[:, None]
    packed = pack(mixed, power_of(top(mixed)))
    mixed = unpack(exchange(jnp.broadcast_to(packed[None], (8, 72, 384)), OCT)).reshape(512, 384)

    cols = ring_gather(cols, place)
    cols = joined_pair(cols, swap(cols, "c"), core)

    cols = cols.astype(jnp.float32) * jnp.exp2(power - 14.0)
    part = dot_wide_left(cols * (right_shift / damp)[None, :], right, ((1,), (0,)))
    update = part + dot_wide_right(left, mixed, ((0,), (0,)))
    update = unpack(exchange(pack(update.reshape(4, 192, 384), power_of(top(update))), QUAD))
    joined_update = jnp.concatenate([update[0], update[1], update[2]], axis=1) + joined_gradient.astype(jnp.float32) / damp / damp
    output_update = update[3] + output_gradient.astype(jnp.float32) / damp / damp
    return joined_update, output_update


def solution(mesh):
    fine = Mesh(mesh.devices.reshape(4, 2, 2, 2, 4, 2, 2), ("yp", "yb", "zp", "zb", "x", "zh", "c"))
    placed = (
        P(FSDP, COL),
        P(FSDP, COL),
        P(FSDP, COL),
        P(COL, FSDP),
        P(FSDP, COL),
        P(COL, FSDP),
        P(),
        P(),
        P(),
        P(),
        P(),
    )
    return jax.shard_map(
        local,
        mesh=fine,
        in_specs=placed,
        out_specs=(P(FSDP, COL), P(FSDP, COL)),
        check_vma=False,
    )
```

```python
import jax
import jax.numpy as jnp
from jax import lax
from jax.sharding import Mesh, PartitionSpec as P

FSDP = ("yp", "yb", "zp", "zb")
COL = ("x", "zh", "c")
QUAD = ("yb", "zb")
OCT = ("yp", "zp")
ROUND = (8, 7)


def shifted(eigen, damp):
    return 1.0 / (eigen + damp) - 1.0 / damp


def exchange(blocks, axes):
    return lax.all_to_all(blocks, axes, 0, 0, tiled=True)


def halves(wide):
    high = lax.reduce_precision(wide, *ROUND)
    return high.astype(jnp.bfloat16), (wide - high).astype(jnp.bfloat16)


def dot_wide_left(wide, narrow, dims):
    high, low = halves(wide)
    dot = lambda part: lax.dot_general(part, narrow, (dims, ((), ())), preferred_element_type=jnp.float32)
    return dot(high) + dot(low)


def dot_wide_right(narrow, wide, dims):
    high, low = halves(wide)
    dot = lambda part: lax.dot_general(narrow, part, (dims, ((), ())), preferred_element_type=jnp.float32)
    return dot(high) + dot(low)


def pack(values, power):
    scaled = (values * jnp.exp2(14.0 - power)).astype(jnp.float16)
    tail = jnp.broadcast_to(power.astype(jnp.float16), values.shape[:-2] + (8, values.shape[-1]))
    return jnp.concatenate([scaled, tail], axis=-2)


def unpack(packed):
    rows = packed.shape[-2] - 8
    power = packed[..., rows : rows + 1, :].astype(jnp.float32)
    return packed[..., :rows, :].astype(jnp.float32) * jnp.exp2(power - 14.0)


def power_of(bound):
    return jnp.clip(jnp.floor(jnp.log2(jnp.maximum(bound, 1e-30))) + 1.0, -100.0, 120.0)


def top(values):
    return jnp.max(jnp.abs(values)).astype(jnp.float32)


def swap(values, axis):
    return lax.ppermute(values, axis, [(0, 1), (1, 0)])


def around(values, axis, size, step):
    return lax.ppermute(values, axis, [(i, (i + step) % size) for i in range(size)])


def ring_gather(values, place):
    held = jnp.stack([values] + [around(values, "x", 4, step) for step in (1, 2, 3)])
    return jnp.concatenate([lax.dynamic_index_in_dim(held, (place - j) % 4, 0, False) for j in range(4)], axis=0)


def core_part(values, core, own):
    half = values.shape[0] // 2
    return lax.dynamic_slice_in_dim(values, (core if own else 1 - core) * half, half, 0)


def joined_pair(mine, other, place):
    first = jnp.where(place == 0, mine, other)
    second = jnp.where(place == 0, other, mine)
    return jnp.concatenate([first, second], axis=0)


def local(
    joined_gradient,
    output_gradient,
    joined_left_basis,
    joined_right_basis,
    output_left_basis,
    output_right_basis,
    joined_left_eigen,
    joined_right_eigen,
    output_left_eigen,
    output_right_eigen,
    damping,
):
    damp = damping[0]
    quad = lax.axis_index("yb") * 2 + lax.axis_index("zb")
    octant = lax.axis_index("yp") * 2 + lax.axis_index("zp")
    core, place = lax.axis_index("c"), lax.axis_index("x")
    is_output = quad == 3
    left_shift = shifted(jnp.where(is_output, output_left_eigen, joined_left_eigen), damp)
    right_shift = shifted(jnp.where(is_output, output_right_eigen, joined_right_eigen), damp)
    left_shift = left_shift.reshape(8, 2, 32).transpose(1, 0, 2).reshape(512)
    right_shift = right_shift.reshape(4, 2, 2, 2, 16).transpose(2, 0, 1, 3, 4)
    right_shift = jnp.where(lax.axis_index("zp") == 1, right_shift[::-1], right_shift).reshape(512)
    own_shift = lax.dynamic_slice_in_dim(left_shift, octant * 64, 64, 0)

    left_j, left_o = joined_left_basis.T, output_left_basis.T
    left = jnp.stack([left_j, left_j, left_j, left_o])
    left = jnp.broadcast_to(left[:, None], (4, 8, 32, 192)).reshape(32, 32, 192)
    left = exchange(left, QUAD + ("x", "zh")).reshape(4, 256, 192)
    left = jnp.concatenate([left[0], left[1], left[2], left[3]], axis=1)
    left = lax.all_gather(left, "c", axis=0, tiled=True)

    right = jnp.concatenate([joined_right_basis.T, output_right_basis.T], axis=1)
    gradients = (joined_gradient[:, :384], joined_gradient[:, 384:768], joined_gradient[:, 768:], output_gradient)
    sent = jnp.stack(
        [jnp.concatenate([block, right[:, 384 * j : 384 * j + 384]], axis=0) for j, block in enumerate(gradients)]
    )
    got = [lax.dynamic_index_in_dim(sent, quad, 0, False)]
    for mask in (1, 2, 3):
        block = lax.dynamic_index_in_dim(sent, quad ^ mask, 0, False)
        got.append(lax.ppermute(block, QUAD, [(i, i ^ mask) for i in range(4)]))
    got = jnp.stack(got)
    got = jnp.stack([lax.dynamic_index_in_dim(got, quad ^ j, 0, False) for j in range(4)])
    gradient = got[:, :192].reshape(768, 384)
    right = got[:, 192:].reshape(64, 384)
    right = exchange(jnp.broadcast_to(right[None], (4, 64, 384)), "yp").reshape(256, 384)
    right = jnp.concatenate([right, swap(right, "zp")], axis=0)
    most = top(gradient)

    rows = jnp.dot(left, gradient, preferred_element_type=jnp.float32)
    rows = pack(rows.reshape(8, 64, 384), power_of(most * 60.0))
    rows = jnp.sum(unpack(exchange(rows, OCT)), axis=0)

    cols = lax.dot_general(gradient, right, (((1,), (1,)), ((), ())), preferred_element_type=jnp.float32)
    cols = core_part(cols, core, True) + swap(core_part(cols, core, False), "c")
    cols = cols.reshape(4, 96, 512)

    mid = dot_wide_left(rows, right, ((1,), (1,)))
    other = jnp.concatenate([core_part(mid, core, False), jnp.broadcast_to(most, (8, 512))], axis=0)
    other = swap(other, "c")
    mid = (core_part(mid, core, True) + other[:32]) / 512.0
    power = power_of(jnp.maximum(most, other[32, 0]) * 864.0)
    both = jnp.concatenate([jnp.broadcast_to(mid[None], (4, 32, 512)), cols], axis=1)
    both = exchange(pack(both, power), "x")
    power = jnp.max(both[:, 128, 0]).astype(jnp.float32)
    both = jnp.sum(unpack(both), axis=0)
    got = swap(pack(both, power), "zh")
    power = jnp.maximum(power, got[128, 0].astype(jnp.float32))
    both = both + unpack(got)
    both = exchange(jnp.broadcast_to(pack(both, power)[None], (4, 136, 512)), QUAD)
    power = jnp.max(both[:, 128, 0]).astype(jnp.float32)
    same = (lax.broadcasted_iota(jnp.int32, (4, 1, 1), 0) == 3) == is_output
    both = jnp.sum(jnp.where(same, unpack(both), 0.0), axis=0)
    mid = lax.all_gather(both[:32], "c", axis=0, tiled=True) * 512.0
    cols = (both[32:] * jnp.exp2(14.0 - power)).astype(jnp.float16)
    mixed = rows / damp + dot_wide_left(mid * right_shift[None, :], right, ((1,), (0,)))
    mixed = mixed * own_shift[:, None]
    packed = pack(mixed, power_of(top(mixed)))
    cols = cols + packed[:1, :1] * 0
    mixed = unpack(exchange(jnp.broadcast_to(packed[None], (8, 72, 384)), OCT)).reshape(512, 384)

    cols = ring_gather(cols, place)
    cols = joined_pair(cols, swap(cols, "c"), core)

    cols = cols.astype(jnp.float32) * jnp.exp2(power - 14.0)
    part = dot_wide_left(cols * (right_shift / damp)[None, :], right, ((1,), (0,)))
    update = part + dot_wide_right(left, mixed, ((0,), (0,)))
    update = unpack(exchange(pack(update.reshape(4, 192, 384), power_of(top(update))), QUAD))
    joined_update = jnp.concatenate([update[0], update[1], update[2]], axis=1) + joined_gradient.astype(jnp.float32) / damp / damp
    output_update = update[3] + output_gradient.astype(jnp.float32) / damp / damp
    return joined_update, output_update


def solution(mesh):
    fine = Mesh(mesh.devices.reshape(4, 2, 2, 2, 4, 2, 2), ("yp", "yb", "zp", "zb", "x", "zh", "c"))
    placed = (
        P(FSDP, COL),
        P(FSDP, COL),
        P(FSDP, COL),
        P(COL, FSDP),
        P(FSDP, COL),
        P(COL, FSDP),
        P(),
        P(),
        P(),
        P(),
        P(),
    )
    return jax.shard_map(
        local,
        mesh=fine,
        in_specs=placed,
        out_specs=(P(FSDP, COL), P(FSDP, COL)),
        check_vma=False,
    )
```

```python
import jax
import jax.numpy as jnp
from jax import lax
from jax.sharding import Mesh, PartitionSpec as P

FSDP = ("yp", "yb", "zp", "zb")
COL = ("x", "zh", "c")
QUAD = ("yb", "zb")
OCT = ("yp", "zp")
ROUND = (8, 7)


def shifted(eigen, damp):
    return 1.0 / (eigen + damp) - 1.0 / damp


def exchange(blocks, axes):
    return lax.all_to_all(blocks, axes, 0, 0, tiled=True)


def halves(wide):
    high = lax.reduce_precision(wide, *ROUND)
    return high.astype(jnp.bfloat16), (wide - high).astype(jnp.bfloat16)


def dot_wide_left(wide, narrow, dims):
    high, low = halves(wide)
    dot = lambda part: lax.dot_general(part, narrow, (dims, ((), ())), preferred_element_type=jnp.float32)
    return dot(high) + dot(low)


def dot_wide_right(narrow, wide, dims):
    high, low = halves(wide)
    dot = lambda part: lax.dot_general(narrow, part, (dims, ((), ())), preferred_element_type=jnp.float32)
    return dot(high) + dot(low)


def pack(values, power):
    scaled = (values * jnp.exp2(14.0 - power)).astype(jnp.float16)
    tail = jnp.broadcast_to(power.astype(jnp.float16), values.shape[:-2] + (8, values.shape[-1]))
    return jnp.concatenate([scaled, tail], axis=-2)


def unpack(packed):
    rows = packed.shape[-2] - 8
    power = packed[..., rows : rows + 1, :].astype(jnp.float32)
    return packed[..., :rows, :].astype(jnp.float32) * jnp.exp2(power - 14.0)


def power_of(bound):
    return jnp.clip(jnp.floor(jnp.log2(jnp.maximum(bound, 1e-30))) + 1.0, -100.0, 120.0)


def top(values):
    return jnp.max(jnp.abs(values)).astype(jnp.float32)


def swap(values, axis):
    return lax.ppermute(values, axis, [(0, 1), (1, 0)])


def around(values, axis, size, step):
    return lax.ppermute(values, axis, [(i, (i + step) % size) for i in range(size)])


def core_part(values, core, own):
    half = values.shape[0] // 2
    return lax.dynamic_slice_in_dim(values, (core if own else 1 - core) * half, half, 0)


def local(
    joined_gradient,
    output_gradient,
    joined_left_basis,
    joined_right_basis,
    output_left_basis,
    output_right_basis,
    joined_left_eigen,
    joined_right_eigen,
    output_left_eigen,
    output_right_eigen,
    damping,
):
    damp = damping[0]
    quad = lax.axis_index("yb") * 2 + lax.axis_index("zb")
    octant = lax.axis_index("yp") * 2 + lax.axis_index("zp")
    core, place = lax.axis_index("c"), lax.axis_index("x")
    is_output = quad == 3
    left_shift = shifted(jnp.where(is_output, output_left_eigen, joined_left_eigen), damp)
    right_shift = shifted(jnp.where(is_output, output_right_eigen, joined_right_eigen), damp)
    left_shift = left_shift.reshape(8, 2, 32).transpose(1, 0, 2).reshape(512)
    right_shift = right_shift.reshape(4, 2, 2, 2, 16).transpose(0, 1, 3, 2, 4).reshape(4, 4, 2, 16)
    right_shift = jnp.where(lax.axis_index("zp") == 1, right_shift[:, :, ::-1], right_shift).reshape(512)
    own_shift = lax.dynamic_slice_in_dim(left_shift, octant * 64, 64, 0)

    left_j, left_o = joined_left_basis.T, output_left_basis.T
    left = jnp.stack([left_j, left_j, left_j, left_o])
    left = jnp.broadcast_to(left[:, None], (4, 8, 32, 192)).reshape(32, 32, 192)
    left = exchange(left, QUAD + ("x", "zh")).reshape(4, 256, 192)
    left = jnp.concatenate([left[0], left[1], left[2], left[3]], axis=1)
    left = lax.all_gather(left, "c", axis=0, tiled=True)

    right = jnp.concatenate([joined_right_basis.T, output_right_basis.T], axis=1)
    right = jnp.concatenate([right, swap(right, "zp")], axis=0)
    right = jnp.stack([right[:, 384 * j : 384 * j + 384] for j in range(4)])
    right = jnp.broadcast_to(right[None], (4, 4, 32, 384)).reshape(16, 32, 384)
    right = exchange(right, ("yp",) + QUAD).reshape(512, 384)

    gradients = (joined_gradient[:, :384], joined_gradient[:, 384:768], joined_gradient[:, 768:], output_gradient)
    sent = jnp.stack(gradients)
    got = [lax.dynamic_index_in_dim(sent, quad, 0, False)]
    for mask in (1, 2, 3):
        block = lax.dynamic_index_in_dim(sent, quad ^ mask, 0, False)
        got.append(lax.ppermute(block, QUAD, [(i, i ^ mask) for i in range(4)]))
    got = jnp.stack(got)
    got = jnp.stack([lax.dynamic_index_in_dim(got, quad ^ j, 0, False) for j in range(4)])
    gradient = got.reshape(768, 384)
    most = top(gradient)

    rows = jnp.dot(left, gradient, preferred_element_type=jnp.float32)
    rows = pack(rows.reshape(8, 64, 384), power_of(most * 60.0))
    rows = jnp.sum(unpack(exchange(rows, OCT)), axis=0)

    cols = lax.dot_general(gradient, right, (((1,), (1,)), ((), ())), preferred_element_type=jnp.float32)
    other = jnp.concatenate([core_part(cols, core, False), jnp.broadcast_to(most, (8, 512))], axis=0)
    other = swap(other, "c")
    power = power_of(jnp.maximum(most, other[384, 0]) * 864.0)
    blocks = pack((core_part(cols, core, True) + other[:384]).reshape(4, 96, 512), power)
    parts = [lax.dynamic_index_in_dim(blocks, place, 0, False)]
    for step in (1, 2, 3):
        parts.append(around(lax.dynamic_index_in_dim(blocks, (place + step) % 4, 0, False), "x", 4, step))
    cols = sum(unpack(part) for part in parts)
    for part in parts[1:]:
        power = jnp.maximum(power, part[96, 0].astype(jnp.float32))

    mid = dot_wide_left(rows, right, ((1,), (1,)))
    mid = core_part(mid, core, True) + swap(core_part(mid, core, False), "c")
    both = jnp.concatenate([mid / 512.0, cols], axis=0)
    got = swap(pack(both, power), "zh")
    power = jnp.maximum(power, got[128, 0].astype(jnp.float32))
    both = both + unpack(got)
    both = exchange(jnp.broadcast_to(pack(both, power)[None], (4, 136, 512)), QUAD)
    power = jnp.max(both[:, 128, 0]).astype(jnp.float32)
    same = (lax.broadcasted_iota(jnp.int32, (4, 1, 1), 0) == 3) == is_output
    both = jnp.sum(jnp.where(same, unpack(both), 0.0), axis=0)
    both = exchange(jnp.broadcast_to(pack(both, power)[None], (4, 136, 512)), "x")
    power = jnp.max(both[:, 128, 0]).astype(jnp.float32)
    mid = jnp.sum(unpack(both)[:, :32], axis=0)
    mid = lax.all_gather(mid, "c", axis=0, tiled=True) * 512.0
    cols = lax.all_gather(both[:, 32:128].reshape(384, 512), "c", axis=0, tiled=True)
    mixed = rows / damp + dot_wide_left(mid * right_shift[None, :], right, ((1,), (0,)))
    mixed = mixed * own_shift[:, None]
    packed = pack(mixed, power_of(top(mixed)))
    mixed = unpack(exchange(jnp.broadcast_to(packed[None], (8, 72, 384)), OCT)).reshape(512, 384)

    cols = cols.astype(jnp.float32) * jnp.exp2(power - 14.0)
    part = dot_wide_left(cols * (right_shift / damp)[None, :], right, ((1,), (0,)))
    update = part + dot_wide_right(left, mixed, ((0,), (0,)))
    update = unpack(exchange(pack(update.reshape(4, 192, 384), power_of(top(update))), QUAD))
    joined_update = jnp.concatenate([update[0], update[1], update[2]], axis=1) + joined_gradient.astype(jnp.float32) / damp / damp
    output_update = update[3] + output_gradient.astype(jnp.float32) / damp / damp
    return joined_update, output_update


def solution(mesh):
    fine = Mesh(mesh.devices.reshape(4, 2, 2, 2, 4, 2, 2), ("yp", "yb", "zp", "zb", "x", "zh", "c"))
    placed = (
        P(FSDP, COL),
        P(FSDP, COL),
        P(FSDP, COL),
        P(COL, FSDP),
        P(FSDP, COL),
        P(COL, FSDP),
        P(),
        P(),
        P(),
        P(),
        P(),
    )
    return jax.shard_map(
        local,
        mesh=fine,
        in_specs=placed,
        out_specs=(P(FSDP, COL), P(FSDP, COL)),
        check_vma=False,
    )
```

```python
import jax
import jax.numpy as jnp
from jax import lax
from jax.sharding import Mesh, PartitionSpec as P

FSDP = ("yp", "yb", "zp", "zb")
COL = ("x", "zh", "c")
QUAD = ("yb", "zb")
OCT = ("yp", "zp")
ROUND = (8, 7)


def shifted(eigen, damp):
    return 1.0 / (eigen + damp) - 1.0 / damp


def exchange(blocks, axes):
    return lax.all_to_all(blocks, axes, 0, 0, tiled=True)


def halves(wide):
    high = lax.reduce_precision(wide, *ROUND)
    return high.astype(jnp.bfloat16), (wide - high).astype(jnp.bfloat16)


def dot_wide_left(wide, narrow, dims):
    high, low = halves(wide)
    dot = lambda part: lax.dot_general(part, narrow, (dims, ((), ())), preferred_element_type=jnp.float32)
    return dot(high) + dot(low)


def dot_wide_right(narrow, wide, dims):
    high, low = halves(wide)
    dot = lambda part: lax.dot_general(narrow, part, (dims, ((), ())), preferred_element_type=jnp.float32)
    return dot(high) + dot(low)


def pack(values, power):
    scaled = (values * jnp.exp2(14.0 - power)).astype(jnp.float16)
    tail = jnp.broadcast_to(power.astype(jnp.float16), values.shape[:-2] + (8, values.shape[-1]))
    return jnp.concatenate([scaled, tail], axis=-2)


def unpack(packed):
    rows = packed.shape[-2] - 8
    power = packed[..., rows : rows + 1, :].astype(jnp.float32)
    return packed[..., :rows, :].astype(jnp.float32) * jnp.exp2(power - 14.0)


def power_of(bound):
    return jnp.clip(jnp.floor(jnp.log2(jnp.maximum(bound, 1e-30))) + 1.0, -100.0, 120.0)


def top(values):
    return jnp.max(jnp.abs(values)).astype(jnp.float32)


def swap(values, axis):
    return lax.ppermute(values, axis, [(0, 1), (1, 0)])


def around(values, axis, size, step):
    return lax.ppermute(values, axis, [(i, (i + step) % size) for i in range(size)])


def core_part(values, core, own):
    half = values.shape[0] // 2
    return lax.dynamic_slice_in_dim(values, (core if own else 1 - core) * half, half, 0)


def local(
    joined_gradient,
    output_gradient,
    joined_left_basis,
    joined_right_basis,
    output_left_basis,
    output_right_basis,
    joined_left_eigen,
    joined_right_eigen,
    output_left_eigen,
    output_right_eigen,
    damping,
):
    damp = damping[0]
    quad = lax.axis_index("yb") * 2 + lax.axis_index("zb")
    octant = lax.axis_index("yp") * 2 + lax.axis_index("zp")
    core = lax.axis_index("c")
    is_output = quad == 3
    left_shift = shifted(jnp.where(is_output, output_left_eigen, joined_left_eigen), damp)
    right_shift = shifted(jnp.where(is_output, output_right_eigen, joined_right_eigen), damp)
    left_shift = left_shift.reshape(4, 2, 2, 32).transpose(2, 0, 1, 3)
    left_shift = jnp.where(lax.axis_index("zh") == 1, left_shift[:, :, ::-1], left_shift).reshape(512)
    own_shift = lax.dynamic_slice_in_dim(left_shift, octant * 64, 64, 0)
    right_shift = right_shift.reshape(4, 2, 2, 2, 16).transpose(0, 1, 3, 2, 4).reshape(4, 4, 2, 16)[::-1]
    right_shift = jnp.where(lax.axis_index("zp") == 1, right_shift[:, :, ::-1], right_shift).reshape(4, 128)
    right_shift = jnp.concatenate([right_shift, right_shift], axis=0)
    right_shift = lax.dynamic_slice_in_dim(right_shift, 3 - lax.axis_index("yp"), 4, 0).reshape(512)

    right = jnp.concatenate([joined_right_basis.T, output_right_basis.T], axis=1)
    right = jnp.concatenate([right, swap(right, "zp")], axis=0)
    lefts = [jnp.concatenate([basis.T[:16], basis.T[16:]], axis=1) for basis in (joined_left_basis, output_left_basis)]
    left = jnp.concatenate(lefts, axis=0)
    other = swap(left, "zh")
    lefts = [jnp.concatenate([left[rows], other[rows]], axis=0) for rows in (slice(0, 16), slice(16, 32))]
    lefts = (lefts[0], lefts[0], lefts[0], lefts[1])
    gradients = (joined_gradient[:, :384], joined_gradient[:, 384:768], joined_gradient[:, 768:], output_gradient)
    sent = jnp.stack(
        [
            jnp.concatenate([gradients[j], right[:, 384 * j : 384 * j + 384], lefts[j]], axis=0)
            for j in range(4)
        ]
    )
    got = exchange(sent, QUAD)
    gradient = got[:, :192].reshape(768, 384)
    most = top(gradient)

    left = got[:, 224:].reshape(4, 2, 16, 384)
    left = jnp.stack([left[..., :192], left[..., 192:]], axis=2).reshape(4, 64, 192)
    left = jnp.concatenate([left[0], left[1], left[2], left[3]], axis=1)
    left = exchange(jnp.broadcast_to(left[None], (4, 64, 768)), "x").reshape(256, 768)
    left = lax.all_gather(left, "c", axis=0, tiled=True)

    right = got[:, 192:224].reshape(128, 384)
    right = jnp.concatenate([right] + [around(right, "yp", 4, step) for step in (1, 2, 3)], axis=0)

    rows = jnp.dot(left, gradient, preferred_element_type=jnp.float32)
    rows = pack(rows.reshape(8, 64, 384), power_of(most * 60.0))
    rows = jnp.sum(unpack(exchange(rows, OCT)), axis=0) * own_shift[:, None]
    rows = pack(rows, power_of(top(rows)))
    rows = exchange(jnp.broadcast_to(rows[None], (8, 72, 384)), OCT)
    limit = jnp.max(rows[:, 64, 0]).astype(jnp.float32)
    limit = most / damp + 40.0 * jnp.exp2(limit)
    rows = unpack(rows).reshape(512, 384)

    lifted = dot_wide_right(left, rows, ((0,), (0,)))
    applied = gradient.astype(jnp.float32) / damp + lifted
    cols = dot_wide_left(applied, right, ((1,), (1,)))
    other = jnp.concatenate([core_part(cols, core, False), jnp.broadcast_to(limit, (8, 512))], axis=0)
    other = swap(other, "c")
    power = power_of(jnp.maximum(limit, other[384, 0]) * 864.0)
    cols = (core_part(cols, core, True) + other[:384]).reshape(4, 96, 512)
    cols = exchange(pack(cols, power), "x")
    power = jnp.max(cols[:, 96, 0]).astype(jnp.float32)
    cols = jnp.sum(unpack(cols), axis=0)
    other = swap(pack(cols, power), "zh")
    power = jnp.maximum(power, other[96, 0].astype(jnp.float32))
    cols = cols + unpack(other)
    cols = exchange(jnp.broadcast_to(pack(cols, power)[None], (4, 104, 512)), QUAD)
    power = jnp.max(cols[:, 96, 0]).astype(jnp.float32)
    same = (lax.broadcasted_iota(jnp.int32, (4, 1, 1), 0) == 3) == is_output
    cols = jnp.sum(jnp.where(same, unpack(cols), 0.0), axis=0)
    cols = (cols * jnp.exp2(14.0 - power)).astype(jnp.float16)
    cols = exchange(jnp.broadcast_to(cols[None], (4, 96, 512)), "x").reshape(384, 512)
    cols = lax.all_gather(cols, "c", axis=0, tiled=True)
    cols = cols.astype(jnp.float32) * jnp.exp2(power - 14.0)

    update = lifted / damp + dot_wide_left(cols * right_shift[None, :], right, ((1,), (0,)))
    update = unpack(exchange(pack(update.reshape(4, 192, 384), power_of(top(update))), QUAD))
    joined_update = jnp.concatenate([update[0], update[1], update[2]], axis=1) + joined_gradient.astype(jnp.float32) / damp / damp
    output_update = update[3] + output_gradient.astype(jnp.float32) / damp / damp
    return joined_update, output_update


def solution(mesh):
    fine = Mesh(mesh.devices.reshape(4, 2, 2, 2, 4, 2, 2), ("yp", "yb", "zp", "zb", "x", "zh", "c"))
    placed = (
        P(FSDP, COL),
        P(FSDP, COL),
        P(FSDP, COL),
        P(COL, FSDP),
        P(FSDP, COL),
        P(COL, FSDP),
        P(),
        P(),
        P(),
        P(),
        P(),
    )
    return jax.shard_map(
        local,
        mesh=fine,
        in_specs=placed,
        out_specs=(P(FSDP, COL), P(FSDP, COL)),
        check_vma=False,
    )
```

```python
import jax
import jax.numpy as jnp
from jax import lax
from jax.sharding import Mesh, PartitionSpec as P

FSDP = ("yp", "yb", "zp", "zb")
COL = ("x", "zh", "c")
QUAD = ("yb", "zb")
OCT = ("yp", "zp")
ROUND = (8, 7)


def shifted(eigen, damp):
    return 1.0 / (eigen + damp) - 1.0 / damp


def exchange(blocks, axes):
    return lax.all_to_all(blocks, axes, 0, 0, tiled=True)


def halves(wide):
    high = lax.reduce_precision(wide, *ROUND)
    return high.astype(jnp.bfloat16), (wide - high).astype(jnp.bfloat16)


def dot_wide_left(wide, narrow, dims):
    high, low = halves(wide)
    dot = lambda part: lax.dot_general(part, narrow, (dims, ((), ())), preferred_element_type=jnp.float32)
    return dot(high) + dot(low)


def dot_wide_right(narrow, wide, dims):
    high, low = halves(wide)
    dot = lambda part: lax.dot_general(narrow, part, (dims, ((), ())), preferred_element_type=jnp.float32)
    return dot(high) + dot(low)


def pack(values):
    top = jnp.max(jnp.abs(values), axis=-2, keepdims=True)
    power = jnp.clip(jnp.floor(jnp.log2(jnp.maximum(top, 1e-30))), -100.0, 120.0)
    scaled = (values * jnp.exp2(14.0 - power)).astype(jnp.float16)
    tail = jnp.broadcast_to(power.astype(jnp.float16), values.shape[:-2] + (8, values.shape[-1]))
    return jnp.concatenate([scaled, tail], axis=-2)


def unpack(packed):
    rows = packed.shape[-2] - 8
    power = packed[..., rows : rows + 1, :].astype(jnp.float32)
    return packed[..., :rows, :].astype(jnp.float32) * jnp.exp2(power - 14.0)


def spread(values, count):
    return jnp.broadcast_to(values[None], (count,) + values.shape)


def swap(values, axis):
    return lax.ppermute(values, axis, [(0, 1), (1, 0)])


def around(values, axis, size, step):
    return lax.ppermute(values, axis, [(i, (i + step) % size) for i in range(size)])


def core_part(values, core, own):
    half = values.shape[0] // 2
    return lax.dynamic_slice_in_dim(values, (core if own else 1 - core) * half, half, 0)


def local(
    joined_gradient,
    output_gradient,
    joined_left_basis,
    joined_right_basis,
    output_left_basis,
    output_right_basis,
    joined_left_eigen,
    joined_right_eigen,
    output_left_eigen,
    output_right_eigen,
    damping,
):
    damp = damping[0]
    quad = lax.axis_index("yb") * 2 + lax.axis_index("zb")
    level = lax.axis_index("yp")
    core = lax.axis_index("c")
    is_output = quad == 3
    left_shift = shifted(jnp.where(is_output, output_left_eigen, joined_left_eigen), damp)
    right_shift = shifted(jnp.where(is_output, output_right_eigen, joined_right_eigen), damp)
    left_shift = left_shift.reshape(4, 2, 2, 32).transpose(2, 0, 1, 3)
    left_shift = jnp.where(lax.axis_index("zh") == 1, left_shift[:, :, ::-1], left_shift).reshape(512)
    own_shift = lax.dynamic_slice_in_dim(left_shift, level * 128, 128, 0)
    right_shift = right_shift.reshape(4, 2, 2, 2, 16).transpose(0, 2, 1, 3, 4).reshape(4, 2, 64)[::-1]
    right_shift = jnp.where(lax.axis_index("zp") == 1, right_shift[:, ::-1], right_shift)
    right_shift = jnp.concatenate([right_shift, right_shift], axis=0)
    right_shift = lax.dynamic_slice_in_dim(right_shift, 3 - level, 4, 0).reshape(512)

    right = jnp.concatenate([joined_right_basis.T, output_right_basis.T], axis=1)
    lefts = [jnp.concatenate([basis.T[:16], basis.T[16:]], axis=1) for basis in (joined_left_basis, output_left_basis)]
    left = jnp.concatenate(lefts, axis=0)
    other = swap(left, "zh")
    lefts = [jnp.concatenate([left[rows], other[rows]], axis=0) for rows in (slice(0, 16), slice(16, 32))]
    lefts = (lefts[0], lefts[0], lefts[0], lefts[1])
    gradients = (joined_gradient[:, :384], joined_gradient[:, 384:768], joined_gradient[:, 768:], output_gradient)
    sent = jnp.stack(
        [
            jnp.concatenate([gradients[j], right[:, 384 * j : 384 * j + 384], lefts[j]], axis=0)
            for j in range(4)
        ]
    )
    got = exchange(sent, QUAD)
    gradient = got[:, :192].reshape(768, 384)

    left = got[:, 208:].reshape(4, 2, 16, 384)
    left = jnp.stack([left[..., :192], left[..., 192:]], axis=2).reshape(4, 64, 192)
    left = jnp.concatenate([left[0], left[1], left[2], left[3]], axis=1)
    left = exchange(spread(left, 4), "x").reshape(256, 768)
    left = lax.all_gather(left, "c", axis=0, tiled=True)

    rows = jnp.dot(left, gradient, preferred_element_type=jnp.float32)
    rows = jnp.sum(unpack(exchange(pack(rows.reshape(4, 128, 384)), "yp")), axis=0)
    right = got[:, 192:208].reshape(64, 384)
    scaled = (right.astype(jnp.float32) * 2.0**19).astype(jnp.float16)
    other = swap(jnp.concatenate([pack(rows), scaled], axis=0), "zp")
    rows = (rows + unpack(other[:136])) * own_shift[:, None]
    rows = unpack(exchange(spread(pack(rows), 4), "yp")).reshape(512, 384)
    scaled = (other[136:].astype(jnp.float32) * 2.0**-19).astype(jnp.bfloat16)
    right = jnp.concatenate([right, scaled], axis=0)
    right = jnp.concatenate([right] + [around(right, "yp", 4, step) for step in (1, 2, 3)], axis=0)

    lifted = dot_wide_right(left, rows, ((0,), (0,)))
    applied = gradient.astype(jnp.float32) / damp + lifted
    cols = dot_wide_left(applied, right, ((1,), (1,)))
    cols = core_part(cols, core, True) + swap(core_part(cols, core, False), "c")
    cols = jnp.sum(unpack(exchange(pack(cols.reshape(4, 96, 512)), "x")), axis=0)
    cols = cols + unpack(swap(pack(cols), "zh"))
    cols = unpack(exchange(spread(pack(cols), 4), QUAD))
    same = (lax.broadcasted_iota(jnp.int32, (4, 1, 1), 0) == 3) == is_output
    cols = jnp.sum(jnp.where(same, cols, 0.0), axis=0)
    cols = exchange(spread(pack(cols), 4), "x")
    cols = unpack(lax.all_gather(cols, "c", axis=0, tiled=True)).reshape(768, 512)

    update = lifted / damp + dot_wide_left(cols * right_shift[None, :], right, ((1,), (0,)))
    update = unpack(exchange(pack(update.reshape(4, 192, 384)), QUAD))
    joined_update = jnp.concatenate([update[0], update[1], update[2]], axis=1) + joined_gradient.astype(jnp.float32) / damp / damp
    output_update = update[3] + output_gradient.astype(jnp.float32) / damp / damp
    return joined_update, output_update


def solution(mesh):
    fine = Mesh(mesh.devices.reshape(4, 2, 2, 2, 4, 2, 2), ("yp", "yb", "zp", "zb", "x", "zh", "c"))
    placed = (
        P(FSDP, COL),
        P(FSDP, COL),
        P(FSDP, COL),
        P(COL, FSDP),
        P(FSDP, COL),
        P(COL, FSDP),
        P(),
        P(),
        P(),
        P(),
        P(),
    )
    return jax.shard_map(
        local,
        mesh=fine,
        in_specs=placed,
        out_specs=(P(FSDP, COL), P(FSDP, COL)),
        check_vma=False,
    )
```

```python
import jax
import jax.numpy as jnp
from jax import lax
from jax.sharding import Mesh, PartitionSpec as P

FSDP = ("yp", "yb", "zp", "zb")
COL = ("x", "zh", "c")
QUAD = ("yb", "zb")
OCT = ("yp", "zp")
ROUND = (8, 7)


def shifted(eigen, damp):
    return 1.0 / (eigen + damp) - 1.0 / damp


def exchange(blocks, axes):
    return lax.all_to_all(blocks, axes, 0, 0, tiled=True)


def halves(wide):
    high = lax.reduce_precision(wide, *ROUND)
    return high.astype(jnp.bfloat16), (wide - high).astype(jnp.bfloat16)


def dot_wide_left(wide, narrow, dims):
    high, low = halves(wide)
    dot = lambda part: lax.dot_general(part, narrow, (dims, ((), ())), preferred_element_type=jnp.float32)
    return dot(high) + dot(low)


def dot_wide_right(narrow, wide, dims):
    high, low = halves(wide)
    dot = lambda part: lax.dot_general(narrow, part, (dims, ((), ())), preferred_element_type=jnp.float32)
    return dot(high) + dot(low)


def pack(values):
    top = jnp.max(jnp.abs(values), axis=-2, keepdims=True)
    power = jnp.clip(jnp.floor(jnp.log2(jnp.maximum(top, 1e-30))), -100.0, 120.0)
    scaled = (values * jnp.exp2(14.0 - power)).astype(jnp.float16)
    tail = jnp.broadcast_to(power.astype(jnp.float16), values.shape[:-2] + (8, values.shape[-1]))
    return jnp.concatenate([scaled, tail], axis=-2)


def unpack(packed):
    rows = packed.shape[-2] - 8
    power = packed[..., rows : rows + 1, :].astype(jnp.float32)
    return packed[..., :rows, :].astype(jnp.float32) * jnp.exp2(power - 14.0)


def spread(values, count):
    return jnp.broadcast_to(values[None], (count,) + values.shape)


def swap(values, axis):
    return lax.ppermute(values, axis, [(0, 1), (1, 0)])


def flip(values, mask):
    return lax.ppermute(values, "yp", [(i, i ^ mask) for i in range(4)])


def core_part(values, core, own):
    half = values.shape[0] // 2
    return lax.dynamic_slice_in_dim(values, (core if own else 1 - core) * half, half, 0)


def local(
    joined_gradient,
    output_gradient,
    joined_left_basis,
    joined_right_basis,
    output_left_basis,
    output_right_basis,
    joined_left_eigen,
    joined_right_eigen,
    output_left_eigen,
    output_right_eigen,
    damping,
):
    damp = damping[0]
    quad = lax.axis_index("yb") * 2 + lax.axis_index("zb")
    level = lax.axis_index("yp")
    core = lax.axis_index("c")
    is_output = quad == 3
    left_shift = shifted(jnp.where(is_output, output_left_eigen, joined_left_eigen), damp)
    right_shift = shifted(jnp.where(is_output, output_right_eigen, joined_right_eigen), damp)
    left_shift = left_shift.reshape(4, 2, 2, 32).transpose(2, 0, 1, 3)
    left_shift = jnp.where(lax.axis_index("zh") == 1, left_shift[:, :, ::-1], left_shift).reshape(512)
    own_shift = lax.dynamic_slice_in_dim(left_shift, level * 128, 128, 0)
    right_shift = right_shift.reshape(2, 2, 2, 2, 2, 16).transpose(0, 3, 1, 2, 4, 5).reshape(2, 2, 2, 64)
    right_shift = jnp.where(level >= 2, right_shift[::-1], right_shift)
    right_shift = jnp.where(lax.axis_index("zp") == 1, right_shift[:, ::-1], right_shift)
    right_shift = jnp.where(level % 2 == 1, right_shift[:, :, ::-1], right_shift).reshape(512)

    right = jnp.concatenate([joined_right_basis.T, output_right_basis.T], axis=1)
    lefts = [jnp.concatenate([basis.T[:16], basis.T[16:]], axis=1) for basis in (joined_left_basis, output_left_basis)]
    left = jnp.concatenate(lefts, axis=0)
    other = swap(left, "zh")
    lefts = [jnp.concatenate([left[rows], other[rows]], axis=0) for rows in (slice(0, 16), slice(16, 32))]
    lefts = (lefts[0], lefts[0], lefts[0], lefts[1])
    gradients = (joined_gradient[:, :384], joined_gradient[:, 384:768], joined_gradient[:, 768:], output_gradient)
    sent = jnp.stack(
        [
            jnp.concatenate([gradients[j], right[:, 384 * j : 384 * j + 384], lefts[j]], axis=0)
            for j in range(4)
        ]
    )
    got = exchange(sent, QUAD)
    gradient = got[:, :192].reshape(768, 384)

    left = got[:, 208:].reshape(4, 2, 16, 384)
    left = jnp.stack([left[..., :192], left[..., 192:]], axis=2).reshape(4, 64, 192)
    left = jnp.concatenate([left[0], left[1], left[2], left[3]], axis=1)
    left = exchange(spread(left, 4), "x").reshape(256, 768)
    left = lax.all_gather(left, "c", axis=0, tiled=True)

    rows = jnp.dot(left, gradient, preferred_element_type=jnp.float32)
    rows = jnp.sum(unpack(exchange(pack(rows.reshape(4, 128, 384)), "yp")), axis=0)
    right = got[:, 192:208].reshape(64, 384)
    right = jnp.concatenate([right, flip(right, 1)], axis=0)
    scaled = (right.astype(jnp.float32) * 2.0**19).astype(jnp.float16)
    other = swap(jnp.concatenate([pack(rows), scaled], axis=0), "zp")
    rows = (rows + unpack(other[:136])) * own_shift[:, None]
    rows = unpack(exchange(spread(pack(rows), 4), "yp")).reshape(512, 384)
    scaled = (other[136:].astype(jnp.float32) * 2.0**-19).astype(jnp.bfloat16)
    right = jnp.concatenate([right, scaled], axis=0)
    right = jnp.concatenate([right, flip(right, 2)], axis=0)

    lifted = dot_wide_right(left, rows, ((0,), (0,)))
    applied = gradient.astype(jnp.float32) / damp + lifted
    cols = dot_wide_left(applied, right, ((1,), (1,)))
    cols = core_part(cols, core, True) + swap(core_part(cols, core, False), "c")
    cols = jnp.sum(unpack(exchange(pack(cols.reshape(4, 96, 512)), "x")), axis=0)
    cols = cols + unpack(swap(pack(cols), "zh"))
    cols = unpack(exchange(spread(pack(cols), 4), QUAD))
    same = (lax.broadcasted_iota(jnp.int32, (4, 1, 1), 0) == 3) == is_output
    cols = jnp.sum(jnp.where(same, cols, 0.0), axis=0)
    cols = exchange(spread(pack(cols), 4), "x")
    cols = unpack(lax.all_gather(cols, "c", axis=0, tiled=True)).reshape(768, 512)

    update = lifted / damp + dot_wide_left(cols * right_shift[None, :], right, ((1,), (0,)))
    update = unpack(exchange(pack(update.reshape(4, 192, 384)), QUAD))
    joined_update = jnp.concatenate([update[0], update[1], update[2]], axis=1) + joined_gradient.astype(jnp.float32) / damp / damp
    output_update = update[3] + output_gradient.astype(jnp.float32) / damp / damp
    return joined_update, output_update


def solution(mesh):
    fine = Mesh(mesh.devices.reshape(4, 2, 2, 2, 4, 2, 2), ("yp", "yb", "zp", "zb", "x", "zh", "c"))
    placed = (
        P(FSDP, COL),
        P(FSDP, COL),
        P(FSDP, COL),
        P(COL, FSDP),
        P(FSDP, COL),
        P(COL, FSDP),
        P(),
        P(),
        P(),
        P(),
        P(),
    )
    return jax.shard_map(
        local,
        mesh=fine,
        in_specs=placed,
        out_specs=(P(FSDP, COL), P(FSDP, COL)),
        check_vma=False,
    )
```

```python
import jax
import jax.numpy as jnp
from jax import lax
from jax.sharding import Mesh, PartitionSpec as P

FSDP = ("yp", "yb", "zp", "zb")
COL = ("x", "zh", "c")
QUAD = ("yb", "zb")
OCT = ("yp", "zp")
ROUND = (8, 7)


def shifted(eigen, damp):
    return 1.0 / (eigen + damp) - 1.0 / damp


def exchange(blocks, axes):
    return lax.all_to_all(blocks, axes, 0, 0, tiled=True)


def halves(wide):
    high = lax.reduce_precision(wide, *ROUND)
    return high.astype(jnp.bfloat16), (wide - high).astype(jnp.bfloat16)


def dot_wide_left(wide, narrow, dims):
    high, low = halves(wide)
    dot = lambda part: lax.dot_general(part, narrow, (dims, ((), ())), preferred_element_type=jnp.float32)
    return dot(high) + dot(low)


def dot_wide_right(narrow, wide, dims):
    high, low = halves(wide)
    dot = lambda part: lax.dot_general(narrow, part, (dims, ((), ())), preferred_element_type=jnp.float32)
    return dot(high) + dot(low)


def pack(values, after=0.0):
    top = jnp.max(jnp.abs(values), axis=-2, keepdims=True)
    power = jnp.clip(jnp.floor(jnp.log2(jnp.maximum(top, 1e-30))), -100.0, 120.0)
    scaled = (values * jnp.exp2(14.0 - power)).astype(jnp.float16)
    tail = jnp.broadcast_to((power + after).astype(jnp.float16), values.shape[:-2] + (8, values.shape[-1]))
    return jnp.concatenate([scaled, tail], axis=-2)


def unpack(packed):
    rows = packed.shape[-2] - 8
    power = packed[..., rows : rows + 1, :].astype(jnp.float32)
    return packed[..., :rows, :].astype(jnp.float32) * jnp.exp2(power - 14.0)


def spread(values, count):
    return jnp.broadcast_to(values[None], (count,) + values.shape)


def swap(values, axis):
    return lax.ppermute(values, axis, [(0, 1), (1, 0)])


def around(values, axis, size, step):
    return lax.ppermute(values, axis, [(i, (i + step) % size) for i in range(size)])


def core_part(values, core, own):
    half = values.shape[0] // 2
    return lax.dynamic_slice_in_dim(values, (core if own else 1 - core) * half, half, 0)


def local(
    joined_gradient,
    output_gradient,
    joined_left_basis,
    joined_right_basis,
    output_left_basis,
    output_right_basis,
    joined_left_eigen,
    joined_right_eigen,
    output_left_eigen,
    output_right_eigen,
    damping,
):
    damp = damping[0]
    quad = lax.axis_index("yb") * 2 + lax.axis_index("zb")
    level = lax.axis_index("yp")
    core = lax.axis_index("c")
    is_output = quad == 3
    left_shift = shifted(jnp.where(is_output, output_left_eigen, joined_left_eigen), damp)
    right_shift = shifted(jnp.where(is_output, output_right_eigen, joined_right_eigen), damp)
    left_shift = left_shift.reshape(4, 2, 2, 32).transpose(2, 0, 1, 3)
    left_shift = jnp.where(lax.axis_index("zh") == 1, left_shift[:, :, ::-1], left_shift).reshape(512)
    own_shift = lax.dynamic_slice_in_dim(left_shift, level * 128, 128, 0)
    right_shift = right_shift.reshape(4, 2, 2, 2, 16).transpose(2, 0, 1, 3, 4).reshape(2, 4, 64)[:, ::-1]
    right_shift = jnp.where(lax.axis_index("zp") == 1, right_shift[::-1], right_shift)
    right_shift = jnp.concatenate([right_shift, right_shift], axis=1)
    right_shift = lax.dynamic_slice_in_dim(right_shift, 3 - level, 4, 1).reshape(512)

    right = jnp.concatenate([joined_right_basis.T, output_right_basis.T], axis=1)
    lefts = [jnp.concatenate([basis.T[:16], basis.T[16:]], axis=1) for basis in (joined_left_basis, output_left_basis)]
    left = jnp.concatenate(lefts, axis=0)
    other = swap(left, "zh")
    lefts = [jnp.concatenate([left[rows], other[rows]], axis=0) for rows in (slice(0, 16), slice(16, 32))]
    lefts = (lefts[0], lefts[0], lefts[0], lefts[1])
    gradients = (joined_gradient[:, :384], joined_gradient[:, 384:768], joined_gradient[:, 768:], output_gradient)
    sent = jnp.stack(
        [
            jnp.concatenate([gradients[j], right[:, 384 * j : 384 * j + 384], lefts[j]], axis=0)
            for j in range(4)
        ]
    )
    got = exchange(sent, QUAD)
    gradient = got[:, :192].reshape(768, 384)

    left = got[:, 208:].reshape(4, 2, 16, 384)
    left = jnp.stack([left[..., :192], left[..., 192:]], axis=2).reshape(4, 64, 192)
    left = jnp.concatenate([left[0], left[1], left[2], left[3]], axis=1)
    left = exchange(spread(left, 4), "x").reshape(256, 768)
    left = lax.all_gather(left, "c", axis=0, tiled=True)

    right = got[:, 192:208].reshape(64, 384)
    parts = [around(right, "yp", 4, step) for step in (1, 2, 3)]
    here = sum(part[0, 0].astype(jnp.float32) for part in parts) * 0.0
    right = jnp.concatenate([right] + parts, axis=0)
    other = swap(right, "zp")
    there = other[0, 0].astype(jnp.float32) * 0.0
    right = jnp.concatenate([right, other], axis=0)

    rows = jnp.dot(left, gradient, preferred_element_type=jnp.float32)
    rows = jnp.sum(unpack(exchange(pack(rows.reshape(4, 128, 384), here), "yp")), axis=0)
    rows = (rows + unpack(swap(pack(rows, there), "zp"))) * own_shift[:, None]
    rows = unpack(exchange(spread(pack(rows), 4), "yp")).reshape(512, 384)

    lifted = dot_wide_right(left, rows, ((0,), (0,)))
    applied = gradient.astype(jnp.float32) / damp + lifted
    cols = dot_wide_left(applied, right, ((1,), (1,)))
    cols = core_part(cols, core, True) + swap(core_part(cols, core, False), "c")
    cols = jnp.sum(unpack(exchange(pack(cols.reshape(4, 96, 512)), "x")), axis=0)
    cols = cols + unpack(swap(pack(cols), "zh"))
    cols = unpack(exchange(spread(pack(cols), 4), QUAD))
    same = (lax.broadcasted_iota(jnp.int32, (4, 1, 1), 0) == 3) == is_output
    cols = jnp.sum(jnp.where(same, cols, 0.0), axis=0)
    cols = exchange(spread(pack(cols), 4), "x")
    cols = unpack(lax.all_gather(cols, "c", axis=0, tiled=True)).reshape(768, 512)

    update = lifted / damp + dot_wide_left(cols * right_shift[None, :], right, ((1,), (0,)))
    update = unpack(exchange(pack(update.reshape(4, 192, 384)), QUAD))
    joined_update = jnp.concatenate([update[0], update[1], update[2]], axis=1) + joined_gradient.astype(jnp.float32) / damp / damp
    output_update = update[3] + output_gradient.astype(jnp.float32) / damp / damp
    return joined_update, output_update


def solution(mesh):
    fine = Mesh(mesh.devices.reshape(4, 2, 2, 2, 4, 2, 2), ("yp", "yb", "zp", "zb", "x", "zh", "c"))
    placed = (
        P(FSDP, COL),
        P(FSDP, COL),
        P(FSDP, COL),
        P(COL, FSDP),
        P(FSDP, COL),
        P(COL, FSDP),
        P(),
        P(),
        P(),
        P(),
        P(),
    )
    return jax.shard_map(
        local,
        mesh=fine,
        in_specs=placed,
        out_specs=(P(FSDP, COL), P(FSDP, COL)),
        check_vma=False,
    )
```

```python
import jax
import jax.numpy as jnp
from jax import lax
from jax.sharding import Mesh, PartitionSpec as P

FSDP = ("yp", "yb", "zp", "zb")
COL = ("x", "zh", "c")
QUAD = ("yb", "zb")
OCT = ("yp", "zp")
ROUND = (8, 7)


def shifted(eigen, damp):
    return 1.0 / (eigen + damp) - 1.0 / damp


def exchange(blocks, axes):
    return lax.all_to_all(blocks, axes, 0, 0, tiled=True)


def halves(wide):
    high = lax.reduce_precision(wide, *ROUND)
    return high.astype(jnp.bfloat16), (wide - high).astype(jnp.bfloat16)


def dot_wide_left(wide, narrow, dims):
    high, low = halves(wide)
    dot = lambda part: lax.dot_general(part, narrow, (dims, ((), ())), preferred_element_type=jnp.float32)
    return dot(high) + dot(low)


def dot_wide_right(narrow, wide, dims):
    high, low = halves(wide)
    dot = lambda part: lax.dot_general(narrow, part, (dims, ((), ())), preferred_element_type=jnp.float32)
    return dot(high) + dot(low)


def pack(values, after=0.0):
    top = jnp.max(jnp.abs(values), axis=-2, keepdims=True)
    power = jnp.clip(jnp.floor(jnp.log2(jnp.maximum(top, 1e-30))), -100.0, 120.0)
    scaled = (values * jnp.exp2(14.0 - power)).astype(jnp.float16)
    tail = jnp.broadcast_to((power + after).astype(jnp.float16), values.shape[:-2] + (8, values.shape[-1]))
    return jnp.concatenate([scaled, tail], axis=-2)


def unpack(packed):
    rows = packed.shape[-2] - 8
    power = packed[..., rows : rows + 1, :].astype(jnp.float32)
    return packed[..., :rows, :].astype(jnp.float32) * jnp.exp2(power - 14.0)


def spread(values, count):
    return jnp.broadcast_to(values[None], (count,) + values.shape)


def swap(values, axis):
    return lax.ppermute(values, axis, [(0, 1), (1, 0)])


def around(values, axis, size, step):
    return lax.ppermute(values, axis, [(i, (i + step) % size) for i in range(size)])


def core_part(values, core, own):
    half = values.shape[0] // 2
    return lax.dynamic_slice_in_dim(values, (core if own else 1 - core) * half, half, 0)


def local(
    joined_gradient,
    output_gradient,
    joined_left_basis,
    joined_right_basis,
    output_left_basis,
    output_right_basis,
    joined_left_eigen,
    joined_right_eigen,
    output_left_eigen,
    output_right_eigen,
    damping,
):
    damp = damping[0]
    quad = lax.axis_index("yb") * 2 + lax.axis_index("zb")
    level = lax.axis_index("yp")
    core = lax.axis_index("c")
    is_output = quad == 3
    left_shift = shifted(jnp.where(is_output, output_left_eigen, joined_left_eigen), damp)
    right_shift = shifted(jnp.where(is_output, output_right_eigen, joined_right_eigen), damp)
    left_shift = left_shift.reshape(4, 2, 2, 32).transpose(2, 0, 1, 3)
    left_shift = jnp.where(lax.axis_index("zh") == 1, left_shift[:, :, ::-1], left_shift).reshape(512)
    own_shift = lax.dynamic_slice_in_dim(left_shift, level * 128, 128, 0)
    right_shift = right_shift.reshape(4, 2, 2, 2, 16).transpose(0, 2, 1, 3, 4).reshape(4, 2, 64)[::-1]
    right_shift = jnp.where(lax.axis_index("zp") == 1, right_shift[:, ::-1], right_shift)
    right_shift = jnp.concatenate([right_shift, right_shift], axis=0)
    right_shift = lax.dynamic_slice_in_dim(right_shift, 3 - level, 4, 0).reshape(512)

    right = jnp.concatenate([joined_right_basis.T, output_right_basis.T], axis=1)
    lefts = [jnp.concatenate([basis.T[:16], basis.T[16:]], axis=1) for basis in (joined_left_basis, output_left_basis)]
    left = jnp.concatenate(lefts, axis=0)
    other = swap(left, "zh")
    lefts = [jnp.concatenate([left[rows], other[rows]], axis=0) for rows in (slice(0, 16), slice(16, 32))]
    lefts = (lefts[0], lefts[0], lefts[0], lefts[1])
    gradients = (joined_gradient[:, :384], joined_gradient[:, 384:768], joined_gradient[:, 768:], output_gradient)
    sent = jnp.stack(
        [
            jnp.concatenate([gradients[j], right[:, 384 * j : 384 * j + 384], lefts[j]], axis=0)
            for j in range(4)
        ]
    )
    got = exchange(sent, QUAD)
    gradient = got[:, :192].reshape(768, 384)

    left = got[:, 208:].reshape(4, 2, 16, 384)
    left = jnp.stack([left[..., :192], left[..., 192:]], axis=2).reshape(4, 64, 192)
    left = jnp.concatenate([left[0], left[1], left[2], left[3]], axis=1)
    left = exchange(spread(left, 4), "x").reshape(256, 768)
    left = lax.all_gather(left, "c", axis=0, tiled=True)

    right = got[:, 192:208].reshape(64, 384)
    other = swap(right, "zp")
    there = other[:1].astype(jnp.float32) * 0.0
    right = jnp.concatenate([right, other], axis=0)

    rows = jnp.dot(left, gradient, preferred_element_type=jnp.float32)
    rows = jnp.sum(unpack(exchange(pack(rows.reshape(4, 128, 384)), "yp")), axis=0)
    rows = (rows + unpack(swap(pack(rows, there), "zp"))) * own_shift[:, None]
    rows = unpack(exchange(spread(pack(rows), 4), "yp")).reshape(512, 384)
    right = jnp.concatenate([right] + [around(right, "yp", 4, step) for step in (1, 2, 3)], axis=0)

    lifted = dot_wide_right(left, rows, ((0,), (0,)))
    applied = gradient.astype(jnp.float32) / damp + lifted
    cols = dot_wide_left(applied, right, ((1,), (1,)))
    cols = core_part(cols, core, True) + swap(core_part(cols, core, False), "c")
    cols = jnp.sum(unpack(exchange(pack(cols.reshape(4, 96, 512)), "x")), axis=0)
    cols = cols + unpack(swap(pack(cols), "zh"))
    cols = unpack(exchange(spread(pack(cols), 4), QUAD))
    same = (lax.broadcasted_iota(jnp.int32, (4, 1, 1), 0) == 3) == is_output
    cols = jnp.sum(jnp.where(same, cols, 0.0), axis=0)
    cols = exchange(spread(pack(cols), 4), "x")
    cols = unpack(lax.all_gather(cols, "c", axis=0, tiled=True)).reshape(768, 512)

    update = lifted / damp + dot_wide_left(cols * right_shift[None, :], right, ((1,), (0,)))
    update = unpack(exchange(pack(update.reshape(4, 192, 384)), QUAD))
    joined_update = jnp.concatenate([update[0], update[1], update[2]], axis=1) + joined_gradient.astype(jnp.float32) / damp / damp
    output_update = update[3] + output_gradient.astype(jnp.float32) / damp / damp
    return joined_update, output_update


def solution(mesh):
    fine = Mesh(mesh.devices.reshape(4, 2, 2, 2, 4, 2, 2), ("yp", "yb", "zp", "zb", "x", "zh", "c"))
    placed = (
        P(FSDP, COL),
        P(FSDP, COL),
        P(FSDP, COL),
        P(COL, FSDP),
        P(FSDP, COL),
        P(COL, FSDP),
        P(),
        P(),
        P(),
        P(),
        P(),
    )
    return jax.shard_map(
        local,
        mesh=fine,
        in_specs=placed,
        out_specs=(P(FSDP, COL), P(FSDP, COL)),
        check_vma=False,
    )
```

```python
import jax
import jax.numpy as jnp
from jax import lax
from jax.sharding import Mesh, PartitionSpec as P

FSDP = ("yp", "yb", "zp", "zb")
COL = ("x", "zh", "c")
QUAD = ("yb", "zb")
OCT = ("yp", "zp")
ROUND = (8, 7)


def shifted(eigen, damp):
    return 1.0 / (eigen + damp) - 1.0 / damp


def exchange(blocks, axes):
    return lax.all_to_all(blocks, axes, 0, 0, tiled=True)


def halves(wide):
    high = lax.reduce_precision(wide, *ROUND)
    return high.astype(jnp.bfloat16), (wide - high).astype(jnp.bfloat16)


def dot_wide_left(wide, narrow, dims):
    high, low = halves(wide)
    dot = lambda part: lax.dot_general(part, narrow, (dims, ((), ())), preferred_element_type=jnp.float32)
    return dot(high) + dot(low)


def dot_wide_right(narrow, wide, dims):
    high, low = halves(wide)
    dot = lambda part: lax.dot_general(narrow, part, (dims, ((), ())), preferred_element_type=jnp.float32)
    return dot(high) + dot(low)


def pack(values):
    top = jnp.max(jnp.abs(values), axis=-2, keepdims=True)
    power = jnp.clip(jnp.floor(jnp.log2(jnp.maximum(top, 1e-30))), -100.0, 120.0)
    scaled = (values * jnp.exp2(14.0 - power)).astype(jnp.float16)
    tail = jnp.broadcast_to(power.astype(jnp.float16), values.shape[:-2] + (8, values.shape[-1]))
    return jnp.concatenate([scaled, tail], axis=-2)


def unpack(packed):
    rows = packed.shape[-2] - 8
    power = packed[..., rows : rows + 1, :].astype(jnp.float32)
    return packed[..., :rows, :].astype(jnp.float32) * jnp.exp2(power - 14.0)


def spread(values, count):
    return jnp.broadcast_to(values[None], (count,) + values.shape)


def swap(values, axis):
    return lax.ppermute(values, axis, [(0, 1), (1, 0)])


def core_part(values, core, own):
    half = values.shape[0] // 2
    return lax.dynamic_slice_in_dim(values, (core if own else 1 - core) * half, half, 0)


def local(
    joined_gradient,
    output_gradient,
    joined_left_basis,
    joined_right_basis,
    output_left_basis,
    output_right_basis,
    joined_left_eigen,
    joined_right_eigen,
    output_left_eigen,
    output_right_eigen,
    damping,
):
    damp = damping[0]
    quad = lax.axis_index("yb") * 2 + lax.axis_index("zb")
    level = lax.axis_index("yp")
    core = lax.axis_index("c")
    is_output = quad == 3
    left_shift = shifted(jnp.where(is_output, output_left_eigen, joined_left_eigen), damp)
    right_shift = shifted(jnp.where(is_output, output_right_eigen, joined_right_eigen), damp)
    left_shift = left_shift.reshape(4, 2, 2, 32).transpose(2, 0, 1, 3)
    left_shift = jnp.where(lax.axis_index("zh") == 1, left_shift[:, :, ::-1], left_shift).reshape(512)
    own_shift = lax.dynamic_slice_in_dim(left_shift, level * 128, 128, 0)
    right_shift = right_shift.reshape(4, 2, 2, 2, 16).transpose(2, 0, 1, 3, 4)
    right_shift = jnp.where(lax.axis_index("zp") == 1, right_shift[::-1], right_shift).reshape(512)

    right = jnp.concatenate([joined_right_basis.T, output_right_basis.T], axis=1)
    lefts = [jnp.concatenate([basis.T[:16], basis.T[16:]], axis=1) for basis in (joined_left_basis, output_left_basis)]
    left = jnp.concatenate(lefts, axis=0)
    other = swap(left, "zh")
    lefts = [jnp.concatenate([left[rows], other[rows]], axis=0) for rows in (slice(0, 16), slice(16, 32))]
    lefts = (lefts[0], lefts[0], lefts[0], lefts[1])
    gradients = (joined_gradient[:, :384], joined_gradient[:, 384:768], joined_gradient[:, 768:], output_gradient)
    sent = jnp.stack(
        [
            jnp.concatenate([gradients[j], right[:, 384 * j : 384 * j + 384], lefts[j]], axis=0)
            for j in range(4)
        ]
    )
    got = exchange(sent, QUAD)
    gradient = got[:, :192].reshape(768, 384)

    left = got[:, 208:].reshape(4, 2, 16, 384)
    left = jnp.stack([left[..., :192], left[..., 192:]], axis=2).reshape(4, 64, 192)
    left = jnp.concatenate([left[0], left[1], left[2], left[3]], axis=1)
    left = exchange(spread(left, 4), "x").reshape(256, 768)
    left = lax.all_gather(left, "c", axis=0, tiled=True)

    right = got[:, 192:208].reshape(64, 384)
    scaled = (right.astype(jnp.float32) * 2.0**19).astype(jnp.float16)

    rows = jnp.dot(left, gradient, preferred_element_type=jnp.float32)
    rows = jnp.concatenate([pack(rows.reshape(4, 128, 384)), spread(scaled, 4)], axis=1)
    got = exchange(rows, "yp")
    rows = jnp.sum(unpack(got[:, :136]), axis=0)
    rows = (rows + unpack(swap(pack(rows), "zp"))) * own_shift[:, None]
    rows = unpack(exchange(spread(pack(rows), 4), "yp")).reshape(512, 384)
    right = (got[:, 136:].reshape(256, 384).astype(jnp.float32) * 2.0**-19).astype(jnp.bfloat16)
    right = jnp.concatenate([right, swap(right, "zp")], axis=0)

    lifted = dot_wide_right(left, rows, ((0,), (0,)))
    applied = gradient.astype(jnp.float32) / damp + lifted
    cols = dot_wide_left(applied, right, ((1,), (1,)))
    cols = core_part(cols, core, True) + swap(core_part(cols, core, False), "c")
    cols = jnp.sum(unpack(exchange(pack(cols.reshape(4, 96, 512)), "x")), axis=0)
    cols = cols + unpack(swap(pack(cols), "zh"))
    cols = unpack(exchange(spread(pack(cols), 4), QUAD))
    same = (lax.broadcasted_iota(jnp.int32, (4, 1, 1), 0) == 3) == is_output
    cols = jnp.sum(jnp.where(same, cols, 0.0), axis=0)
    cols = exchange(spread(pack(cols), 4), "x")
    cols = unpack(lax.all_gather(cols, "c", axis=0, tiled=True)).reshape(768, 512)

    update = lifted / damp + dot_wide_left(cols * right_shift[None, :], right, ((1,), (0,)))
    update = unpack(exchange(pack(update.reshape(4, 192, 384)), QUAD))
    joined_update = jnp.concatenate([update[0], update[1], update[2]], axis=1) + joined_gradient.astype(jnp.float32) / damp / damp
    output_update = update[3] + output_gradient.astype(jnp.float32) / damp / damp
    return joined_update, output_update


def solution(mesh):
    fine = Mesh(mesh.devices.reshape(4, 2, 2, 2, 4, 2, 2), ("yp", "yb", "zp", "zb", "x", "zh", "c"))
    placed = (
        P(FSDP, COL),
        P(FSDP, COL),
        P(FSDP, COL),
        P(COL, FSDP),
        P(FSDP, COL),
        P(COL, FSDP),
        P(),
        P(),
        P(),
        P(),
        P(),
    )
    return jax.shard_map(
        local,
        mesh=fine,
        in_specs=placed,
        out_specs=(P(FSDP, COL), P(FSDP, COL)),
        check_vma=False,
    )
```

```python
import jax
import jax.numpy as jnp
from jax import lax
from jax.sharding import Mesh, PartitionSpec as P

FSDP = ("yp", "yb", "zp", "zb")
COL = ("x", "zh", "c")
QUAD = ("yb", "zb")
OCT = ("yp", "zp")
ROUND = (8, 7)


def shifted(eigen, damp):
    return 1.0 / (eigen + damp) - 1.0 / damp


def exchange(blocks, axes):
    return lax.all_to_all(blocks, axes, 0, 0, tiled=True)


def halves(wide):
    high = lax.reduce_precision(wide, *ROUND)
    return high.astype(jnp.bfloat16), (wide - high).astype(jnp.bfloat16)


def dot(left, right, dims):
    return lax.dot_general(left, right, (dims, ((), ())), preferred_element_type=jnp.float32)


def pack(values):
    top = jnp.max(jnp.abs(values), axis=-2, keepdims=True)
    power = jnp.clip(jnp.floor(jnp.log2(jnp.maximum(top, 1e-30))), -100.0, 120.0)
    scaled = (values * jnp.exp2(14.0 - power)).astype(jnp.float16)
    tail = jnp.broadcast_to(power.astype(jnp.float16), values.shape[:-2] + (8, values.shape[-1]))
    return jnp.concatenate([scaled, tail], axis=-2)


def unpack(packed):
    rows = packed.shape[-2] - 8
    power = packed[..., rows : rows + 1, :].astype(jnp.float32)
    return packed[..., :rows, :].astype(jnp.float32) * jnp.exp2(power - 14.0)


def spread(values, count):
    return jnp.broadcast_to(values[None], (count,) + values.shape)


def swap(values, axis):
    return lax.ppermute(values, axis, [(0, 1), (1, 0)])


def core_part(values, core, own):
    half = values.shape[0] // 2
    return lax.dynamic_slice_in_dim(values, (core if own else 1 - core) * half, half, 0)


def local(
    joined_gradient,
    output_gradient,
    joined_left_basis,
    joined_right_basis,
    output_left_basis,
    output_right_basis,
    joined_left_eigen,
    joined_right_eigen,
    output_left_eigen,
    output_right_eigen,
    damping,
):
    damp = damping[0]
    quad = lax.axis_index("yb") * 2 + lax.axis_index("zb")
    level = lax.axis_index("yp")
    core = lax.axis_index("c")
    is_output = quad == 3
    left_shift = shifted(jnp.where(is_output, output_left_eigen, joined_left_eigen), damp)
    right_shift = shifted(jnp.where(is_output, output_right_eigen, joined_right_eigen), damp)
    left_shift = left_shift.reshape(4, 2, 2, 32).transpose(2, 0, 1, 3)
    left_shift = jnp.where(lax.axis_index("zh") == 1, left_shift[:, :, ::-1], left_shift).reshape(512)
    own_shift = lax.dynamic_slice_in_dim(left_shift, level * 128, 128, 0)
    right_shift = right_shift.reshape(4, 2, 2, 2, 16).transpose(2, 0, 1, 3, 4)
    right_shift = jnp.where(lax.axis_index("zp") == 1, right_shift[::-1], right_shift).reshape(512)

    right = jnp.concatenate([joined_right_basis.T, output_right_basis.T], axis=1)
    lefts = [jnp.concatenate([basis.T[:16], basis.T[16:]], axis=1) for basis in (joined_left_basis, output_left_basis)]
    left = jnp.concatenate(lefts, axis=0)
    other = swap(left, "zh")
    lefts = [jnp.concatenate([left[rows], other[rows]], axis=0) for rows in (slice(0, 16), slice(16, 32))]
    lefts = (lefts[0], lefts[0], lefts[0], lefts[1])
    gradients = (joined_gradient[:, :384], joined_gradient[:, 384:768], joined_gradient[:, 768:], output_gradient)
    sent = jnp.stack(
        [
            jnp.concatenate([gradients[j], right[:, 384 * j : 384 * j + 384], lefts[j]], axis=0)
            for j in range(4)
        ]
    )
    got = exchange(sent, QUAD)
    gradient = got[:, :192].reshape(768, 384)

    left = got[:, 208:].reshape(4, 2, 16, 384)
    left = jnp.stack([left[..., :192], left[..., 192:]], axis=2).reshape(4, 64, 192)
    left = jnp.concatenate([left[0], left[1], left[2], left[3]], axis=1)
    left = exchange(spread(left, 4), "x").reshape(256, 768)
    left = lax.all_gather(left, "c", axis=0, tiled=True)

    right = got[:, 192:208].reshape(64, 384)
    scaled = (right.astype(jnp.float32) * 2.0**19).astype(jnp.float16)

    rows = jnp.dot(left, gradient, preferred_element_type=jnp.float32)
    rows = jnp.concatenate([pack(rows.reshape(4, 128, 384)), spread(scaled, 4)], axis=1)
    got = exchange(rows, "yp")
    rows = jnp.sum(unpack(got[:, :136]), axis=0)
    rows = (rows + unpack(swap(pack(rows), "zp"))) * own_shift[:, None]
    rows = unpack(exchange(spread(pack(rows), 4), "yp")).reshape(512, 384)
    right = (got[:, 136:].reshape(256, 384).astype(jnp.float32) * 2.0**-19).astype(jnp.bfloat16)
    right = jnp.concatenate([right, swap(right, "zp")], axis=0)

    plain = dot(gradient, right, ((1,), (1,))) / damp
    lifted = dot(jnp.concatenate([left, left], axis=0), jnp.concatenate(halves(rows), axis=0), ((0,), (0,)))
    wide = jnp.concatenate([right, right], axis=1)
    cols = plain + dot(jnp.concatenate(halves(lifted), axis=1), wide, ((1,), (1,)))
    cols = core_part(cols, core, True) + swap(core_part(cols, core, False), "c")
    cols = jnp.sum(unpack(exchange(pack(cols.reshape(4, 96, 512)), "x")), axis=0)
    cols = cols + unpack(swap(pack(cols), "zh"))
    cols = unpack(exchange(spread(pack(cols), 4), QUAD))
    same = (lax.broadcasted_iota(jnp.int32, (4, 1, 1), 0) == 3) == is_output
    cols = jnp.sum(jnp.where(same, cols, 0.0), axis=0)
    cols = exchange(spread(pack(cols), 4), "x")
    cols = unpack(lax.all_gather(cols, "c", axis=0, tiled=True)).reshape(768, 512)

    cols = jnp.concatenate(halves(cols * right_shift[None, :]), axis=1)
    update = lifted / damp + dot(cols, jnp.concatenate([right, right], axis=0), ((1,), (0,)))
    update = unpack(exchange(pack(update.reshape(4, 192, 384)), QUAD))
    joined_update = jnp.concatenate([update[0], update[1], update[2]], axis=1) + joined_gradient.astype(jnp.float32) / damp / damp
    output_update = update[3] + output_gradient.astype(jnp.float32) / damp / damp
    return joined_update, output_update


def solution(mesh):
    fine = Mesh(mesh.devices.reshape(4, 2, 2, 2, 4, 2, 2), ("yp", "yb", "zp", "zb", "x", "zh", "c"))
    placed = (
        P(FSDP, COL),
        P(FSDP, COL),
        P(FSDP, COL),
        P(COL, FSDP),
        P(FSDP, COL),
        P(COL, FSDP),
        P(),
        P(),
        P(),
        P(),
        P(),
    )
    return jax.shard_map(
        local,
        mesh=fine,
        in_specs=placed,
        out_specs=(P(FSDP, COL), P(FSDP, COL)),
        check_vma=False,
    )
```

```python
import jax
import jax.numpy as jnp
from jax import lax
from jax.sharding import Mesh, PartitionSpec as P

FSDP = ("yp", "yb", "zp", "zb")
COL = ("x", "zh", "c")
QUAD = ("yb", "zb")
OCT = ("yp", "zp")
ROUND = (8, 7)


def shifted(eigen, damp):
    return 1.0 / (eigen + damp) - 1.0 / damp


def exchange(blocks, axes):
    return lax.all_to_all(blocks, axes, 0, 0, tiled=True)


def halves(wide):
    high = lax.reduce_precision(wide, *ROUND)
    return high.astype(jnp.bfloat16), (wide - high).astype(jnp.bfloat16)


def dot_wide_left(wide, narrow, dims):
    high, low = halves(wide)
    dot = lambda part: lax.dot_general(part, narrow, (dims, ((), ())), preferred_element_type=jnp.float32)
    return dot(high) + dot(low)


def dot_wide_right(narrow, wide, dims):
    high, low = halves(wide)
    dot = lambda part: lax.dot_general(narrow, part, (dims, ((), ())), preferred_element_type=jnp.float32)
    return dot(high) + dot(low)


def pack(values, after=0.0):
    top = jnp.max(jnp.abs(values), axis=-2, keepdims=True)
    power = jnp.clip(jnp.floor(jnp.log2(jnp.maximum(top, 1e-30))), -100.0, 120.0)
    scaled = (values * jnp.exp2(14.0 - power)).astype(jnp.float16)
    tail = jnp.broadcast_to((power + after).astype(jnp.float16), values.shape[:-2] + (8, values.shape[-1]))
    return jnp.concatenate([scaled, tail], axis=-2)


def unpack(packed):
    rows = packed.shape[-2] - 8
    power = packed[..., rows : rows + 1, :].astype(jnp.float32)
    return packed[..., :rows, :].astype(jnp.float32) * jnp.exp2(power - 14.0)


def spread(values, count):
    return jnp.broadcast_to(values[None], (count,) + values.shape)


def swap(values, axis):
    return lax.ppermute(values, axis, [(0, 1), (1, 0)])


def around(values, axis, size, step):
    return lax.ppermute(values, axis, [(i, (i + step) % size) for i in range(size)])


def core_part(values, core, own):
    half = values.shape[0] // 2
    return lax.dynamic_slice_in_dim(values, (core if own else 1 - core) * half, half, 0)


def local(
    joined_gradient,
    output_gradient,
    joined_left_basis,
    joined_right_basis,
    output_left_basis,
    output_right_basis,
    joined_left_eigen,
    joined_right_eigen,
    output_left_eigen,
    output_right_eigen,
    damping,
):
    damp = damping[0]
    quad = lax.axis_index("yb") * 2 + lax.axis_index("zb")
    level = lax.axis_index("yp")
    octant = level * 2 + lax.axis_index("zp")
    core = lax.axis_index("c")
    is_output = quad == 3
    left_shift = shifted(jnp.where(is_output, output_left_eigen, joined_left_eigen), damp)
    right_shift = shifted(jnp.where(is_output, output_right_eigen, joined_right_eigen), damp)
    left_shift = left_shift.reshape(4, 2, 2, 32).transpose(2, 0, 1, 3)
    left_shift = jnp.where(lax.axis_index("zh") == 1, left_shift[:, :, ::-1], left_shift).reshape(512)
    own_shift = lax.dynamic_slice_in_dim(left_shift, octant * 64, 64, 0)
    right_shift = right_shift.reshape(4, 2, 2, 2, 16).transpose(0, 2, 1, 3, 4).reshape(4, 2, 64)[::-1]
    right_shift = jnp.where(lax.axis_index("zp") == 1, right_shift[:, ::-1], right_shift)
    right_shift = jnp.concatenate([right_shift, right_shift], axis=0)
    right_shift = lax.dynamic_slice_in_dim(right_shift, 3 - level, 4, 0).reshape(512)

    right = jnp.concatenate([joined_right_basis.T, output_right_basis.T], axis=1)
    lefts = [jnp.concatenate([basis.T[:16], basis.T[16:]], axis=1) for basis in (joined_left_basis, output_left_basis)]
    left = jnp.concatenate(lefts, axis=0)
    other = swap(left, "zh")
    lefts = [jnp.concatenate([left[rows], other[rows]], axis=0) for rows in (slice(0, 16), slice(16, 32))]
    lefts = (lefts[0], lefts[0], lefts[0], lefts[1])
    gradients = (joined_gradient[:, :384], joined_gradient[:, 384:768], joined_gradient[:, 768:], output_gradient)
    sent = jnp.stack(
        [
            jnp.concatenate([gradients[j], right[:, 384 * j : 384 * j + 384], lefts[j]], axis=0)
            for j in range(4)
        ]
    )
    got = exchange(sent, QUAD)
    gradient = got[:, :192].reshape(768, 384)

    left = got[:, 208:].reshape(4, 2, 16, 384)
    left = jnp.stack([left[..., :192], left[..., 192:]], axis=2).reshape(4, 64, 192)
    left = jnp.concatenate([left[0], left[1], left[2], left[3]], axis=1)
    left = exchange(spread(left, 4), "x").reshape(256, 768)
    left = lax.all_gather(left, "c", axis=0, tiled=True)

    right = got[:, 192:208].reshape(64, 384)
    other = swap(right, "zp")
    there = other[:1].astype(jnp.float32) * 0.0
    right = jnp.concatenate([right, other], axis=0)

    rows = jnp.dot(left, gradient, preferred_element_type=jnp.float32)
    rows = jnp.sum(unpack(exchange(pack(rows.reshape(8, 64, 384)), OCT)), axis=0)
    rows = pack(rows * own_shift[:, None], there)
    rows = unpack(exchange(spread(rows, 8), OCT)).reshape(512, 384)
    right = jnp.concatenate([right] + [around(right, "yp", 4, step) for step in (1, 2, 3)], axis=0)

    lifted = dot_wide_right(left, rows, ((0,), (0,)))
    applied = gradient.astype(jnp.float32) / damp + lifted
    cols = dot_wide_left(applied, right, ((1,), (1,)))
    cols = core_part(cols, core, True) + swap(core_part(cols, core, False), "c")
    cols = jnp.sum(unpack(exchange(pack(cols.reshape(4, 96, 512)), "x")), axis=0)
    cols = cols + unpack(swap(pack(cols), "zh"))
    cols = unpack(exchange(spread(pack(cols), 4), QUAD))
    same = (lax.broadcasted_iota(jnp.int32, (4, 1, 1), 0) == 3) == is_output
    cols = jnp.sum(jnp.where(same, cols, 0.0), axis=0)
    cols = exchange(spread(pack(cols), 4), "x")
    cols = unpack(lax.all_gather(cols, "c", axis=0, tiled=True)).reshape(768, 512)

    update = lifted / damp + dot_wide_left(cols * right_shift[None, :], right, ((1,), (0,)))
    update = unpack(exchange(pack(update.reshape(4, 192, 384)), QUAD))
    joined_update = jnp.concatenate([update[0], update[1], update[2]], axis=1) + joined_gradient.astype(jnp.float32) / damp / damp
    output_update = update[3] + output_gradient.astype(jnp.float32) / damp / damp
    return joined_update, output_update


def solution(mesh):
    fine = Mesh(mesh.devices.reshape(4, 2, 2, 2, 4, 2, 2), ("yp", "yb", "zp", "zb", "x", "zh", "c"))
    placed = (
        P(FSDP, COL),
        P(FSDP, COL),
        P(FSDP, COL),
        P(COL, FSDP),
        P(FSDP, COL),
        P(COL, FSDP),
        P(),
        P(),
        P(),
        P(),
        P(),
    )
    return jax.shard_map(
        local,
        mesh=fine,
        in_specs=placed,
        out_specs=(P(FSDP, COL), P(FSDP, COL)),
        check_vma=False,
    )
```
